32 devices in a mesh: slot: 16 (over z, y, core), blk: 2 (over x).
Axes of the slice: x: 2, y: 2, z: 4, core: 2. Of those that a mesh axis runs over, the one named last changes fastest.
Arguments:
- atom_feats: bfloat16 [48, 512, 512], P('slot', 'blk'), may hold values from -6 to 6
- pair_feats: bfloat16 [48, 64, 512, 512], P('slot', None, 'blk'), may hold values from -6 to 6
- type_ids: int32 [48, 512], P('slot', 'blk'), may hold values from 0 to 31
- mol_lengths: int32 [48, 4], P('slot'), may hold values from 1 to 509, as said below
- type_table: float32 [32, 512], replicated, may hold values from -4 to 4
- ln1_gain: float32 [512], replicated, may hold values from 0.5 to 1.5
- ln1_shift: float32 [512], replicated, may hold values from -1 to 1
- w_query: bfloat16 [512, 512], replicated, may hold values from -0.25 to 0.25
- b_query: float32 [512], replicated, may hold values from -1.5 to 1.5
- w_key: bfloat16 [512, 512], replicated, may hold values from -0.25 to 0.25
- w_value: bfloat16 [512, 512], replicated, may hold values from -0.25 to 0.25
- b_value: float32 [512], replicated, may hold values from -1.5 to 1.5
- w_out: bfloat16 [512, 512], replicated, may hold values from -2 to 2
- b_out: float32 [512], replicated, may hold values from -1.5 to 1.5
- ln2_gain: float32 [512], replicated, may hold values from 0.5 to 1.5
- ln2_shift: float32 [512], replicated, may hold values from -1 to 1
- w_up: bfloat16 [512, 2048], replicated, may hold values from -0.25 to 0.25
- b_up: float32 [2048], replicated, may hold values from -1.5 to 1.5
- w_down: bfloat16 [2048, 512], replicated, may hold values from -0.125 to 0.125
- b_down: float32 [512], replicated, may hold values from -1.5 to 1.5
- atom_cotan: bfloat16 [48, 512, 512], P('slot', 'blk'), may hold values from -6 to 6
- pair_cotan: bfloat16 [48, 64, 512, 512], P('slot', None, 'blk'), may hold values from -6 to 6
Outputs:
- atom_out: bfloat16 [48, 512, 512], P('slot', 'blk')
- pair_out: bfloat16 [48, 64, 512, 512], P('slot', None, 'blk')
- penalty: float32 [], replicated
- atom_grad: bfloat16 [48, 512, 512], P('slot', 'blk')
- pair_grad: bfloat16 [48, 64, 512, 512], P('slot', None, 'blk')
- g_type_table: float32 [32, 512], replicated
- g_ln1_gain: float32 [512], replicated
- g_ln1_shift: float32 [512], replicated
- g_w_query: float32 [512, 512], replicated
- g_b_query: float32 [512], replicated
- g_w_key: float32 [512, 512], replicated
- g_w_value: float32 [512, 512], replicated
- g_b_value: float32 [512], replicated
- g_w_out: float32 [512, 512], replicated
- g_b_out: float32 [512], replicated
- g_ln2_gain: float32 [512], replicated
- g_ln2_shift: float32 [512], replicated
- g_w_up: float32 [512, 2048], replicated
- g_b_up: float32 [2048], replicated
- g_w_down: float32 [2048, 512], replicated
- g_b_down: float32 [512], replicated
The draws below stay inside these ranges and needn't reach their ends.
Inputs may be any that keep to these rules, and one draw needn't show every extreme that they name: `mol_lengths`: each slot holds 4 molecules that fill its 512 atoms in order with no padding; one of them, at a place drawn per slot, covers from the slot's first block of 256 atoms to its last, and the others have at most (255) // 3 atoms each. In the first slot the others have one atom each.
All inputs are finite; a program needn't handle non-finite values.
Results may differ from the reference program's by a relative error of at most 0.007.
The reference program's roundings to bfloat16 on the way count: a program that leaves them out, or rounds other values in their place, can miss the bound.
Values may be sent and summed in bfloat16 or wider, within the bound.
No kernel may reach another device: no remote copies, remote signals or barrier semaphores. Data moves between devices by JAX's collectives and lax.ppermute only.
A program may use at most 640 MiB of HBM per device.

```python
import jax
import jax.numpy as jnp
from jax import lax

D = 512
H = 64
HEAD = 8
FF = 2048
TYPES = 32
SLOT_LEN = 512
MOLS = 4
SLOTS = 48
ROWS_BLK = 256


def draw_mol_lengths(key, part):
    key = jax.random.fold_in(key, 11)
    small_key, place_key = jax.random.split(key)
    smalls = jax.random.randint(small_key, (SLOTS, MOLS - 1), 1, (ROWS_BLK - 1) // 3 + 1).astype(jnp.int32)
    first_row = (jnp.arange(SLOTS, dtype=jnp.int32) == 0)[:, None]
    smalls = jnp.where(first_row, jnp.ones_like(smalls), smalls).astype(jnp.int32)
    place = jax.random.randint(place_key, (SLOTS, 1), 0, MOLS).astype(jnp.int32)
    largest = SLOT_LEN - jnp.sum(smalls, axis=1, keepdims=True)
    zeros = jnp.zeros((SLOTS, 1), jnp.int32)
    ahead = jnp.concatenate([smalls, zeros], axis=1)
    behind = jnp.concatenate([zeros, smalls], axis=1)
    column = jnp.arange(MOLS, dtype=jnp.int32)[None, :]
    return jnp.where(column < place, ahead, jnp.where(column == place, largest, behind)).astype(jnp.int32)


def with_ends(result, key, smallest, high):
    spot = [jax.random.randint(jax.random.fold_in(key, axis), (), 0, length) for axis, length in enumerate(result.shape)]
    main_axis = result.shape.index(max(result.shape))
    beside = spot[:main_axis] + [(spot[main_axis] + 1) % result.shape[main_axis]] + spot[main_axis + 1:]
    return result.at[tuple(spot)].set(smallest).at[tuple(beside)].set(high)


def levels(key, extent, pieces, least, high):
    level = 1.0
    for axis_at, blocks in pieces:
        heights = jax.random.uniform(jax.random.fold_in(jax.random.fold_in(key, 6), axis_at), (blocks,), jnp.float32, least / len(pieces), high / len(pieces))
        level = level * jnp.repeat(jnp.exp(heights), extent[axis_at] // blocks).reshape((-1,) + (1,) * (len(extent) - 1 - axis_at))
    return level


def bell_draw(rng, shape, width, reach, shards=(), kind=jnp.bfloat16):
    entries = width * jax.random.normal(rng, shape, jnp.float32)
    if shards:
        entries = entries * levels(rng, shape, shards, -0.22, 0.18)
    return jnp.clip(entries, -reach, reach).astype(kind)


def setup_inputs(seed: int = 0) -> dict:
    key_of = jax.random.split(jax.random.key(seed), 23)
    return {
        "atom_feats": bell_draw(key_of[0], (SLOTS, SLOT_LEN, D), 1.0, 6.0, ((0, 16), (1, 2))),
        "pair_feats": bell_draw(key_of[1], (SLOTS, H, SLOT_LEN, SLOT_LEN), 1.0, 6.0, ((0, 16), (2, 2))),
        "type_ids": with_ends(jax.random.randint(key_of[2], (SLOTS, SLOT_LEN), 0, TYPES), jax.random.fold_in(key_of[2], 1), 0, TYPES - 1).astype(jnp.int32),
        "mol_lengths": draw_mol_lengths(jax.random.fold_in(key_of[22], 71), 0),
        "type_table": bell_draw(key_of[4], (TYPES, D), 0.5, 4.0, (), jnp.float32),
        "ln1_gain": jnp.clip(1.0 + 0.1 * jax.random.normal(key_of[5], (D,), jnp.float32), 0.5, 1.5),
        "ln1_shift": bell_draw(key_of[6], (D,), 0.2, 1.0, (), jnp.float32),
        "w_query": bell_draw(key_of[7], (D, D), D ** -0.5, 0.25),
        "b_query": bell_draw(key_of[8], (D,), 0.3, 1.5, (), jnp.float32),
        "w_key": bell_draw(key_of[9], (D, D), D ** -0.5, 0.25),
        "w_value": bell_draw(key_of[10], (D, D), D ** -0.5, 0.25),
        "b_value": bell_draw(key_of[11], (D,), 0.3, 1.5, (), jnp.float32),
        "w_out": bell_draw(key_of[12], (D, D), (D // 64) ** -0.5, 2.0),
        "b_out": bell_draw(key_of[13], (D,), 0.3, 1.5, (), jnp.float32),
        "ln2_gain": jnp.clip(1.0 + 0.1 * jax.random.normal(key_of[14], (D,), jnp.float32), 0.5, 1.5),
        "ln2_shift": bell_draw(key_of[15], (D,), 0.2, 1.0, (), jnp.float32),
        "w_up": bell_draw(key_of[16], (D, FF), D ** -0.5, 0.25),
        "b_up": bell_draw(key_of[17], (FF,), 0.3, 1.5, (), jnp.float32),
        "w_down": bell_draw(key_of[18], (FF, D), FF ** -0.5, 0.125),
        "b_down": bell_draw(key_of[19], (D,), 0.3, 1.5, (), jnp.float32),
        "atom_cotan": bell_draw(key_of[20], (SLOTS, SLOT_LEN, D), 1.0, 6.0, ((0, 16), (1, 2))),
        "pair_cotan": bell_draw(key_of[21], (SLOTS, H, SLOT_LEN, SLOT_LEN), 1.0, 6.0, ((0, 16), (2, 2))),
    }


@jax.custom_vjp
def low(v):
    return lax.optimization_barrier(v.astype(jnp.bfloat16)).astype(jnp.float32)

@jax.custom_vjp
def low_back(v):
    return v

def low_keep(v):
    return (low(v), None)

def low_pass(kept, grad):
    return (grad,)

def back_keep(v):
    return (v, None)

def back_low(kept, grad):
    return (low(grad),)
low.defvjp(low_keep, low_pass)
low_back.defvjp(back_keep, back_low)
EPSILON = 1e-05
HIGHEST = lax.Precision.HIGHEST

def matmul(left, right):
    return jnp.dot(left, right, precision=HIGHEST)

def layer_norm(values, gain, shift):
    center = values - lax.optimization_barrier(jnp.mean(values, axis=-1, keepdims=True))
    spread = lax.optimization_barrier(jnp.mean(center * center, axis=-1, keepdims=True))
    return center * lax.rsqrt(spread + EPSILON) * gain + shift

def molecule_ids(length_row):
    bounds = jnp.cumsum(length_row).astype(jnp.int32)
    places = jnp.arange(SLOT_LEN, dtype=jnp.int32)
    return lax.optimization_barrier(jnp.sum((places[:, None] >= bounds[None, :]).astype(jnp.int32), axis=1))

def slot_layer(params, atom_slot, pair_slot, type_slot, length_slot, pair_total):
    type_table, ln1_gain, ln1_shift, w_query, b_query, w_key, w_value, b_value, w_out, b_out, ln2_gain, ln2_shift, w_up, b_up, w_down, b_down = params
    base = atom_slot + jnp.take(type_table, type_slot, axis=0)
    normed1 = low(layer_norm(base, ln1_gain, ln1_shift))
    query = low(low_back(matmul(normed1, w_query) + b_query))
    keyed = low(low_back(matmul(normed1, w_key)))
    valued = low(low_back(matmul(normed1, w_value) + b_value))
    query_head_split = query.reshape(SLOT_LEN, H, HEAD)
    key_head_split = keyed.reshape(SLOT_LEN, H, HEAD)
    value_head_split = valued.reshape(SLOT_LEN, H, HEAD)
    logits = jnp.einsum('ihd,jhd->hij', query_head_split, key_head_split, precision=HIGHEST) * HEAD ** (-0.5) + pair_slot
    logits = low_back(logits)
    mol_id = molecule_ids(length_slot)
    pair_mask = (mol_id[:, None] == mol_id[None, :])[None, :, :]
    masked = jnp.where(pair_mask, logits, -1000000000.0)
    row_top = lax.optimization_barrier(jnp.max(masked, axis=-1, keepdims=True))
    exponent = jnp.exp(masked - row_top)
    probs = exponent / lax.optimization_barrier(jnp.sum(exponent, axis=-1, keepdims=True))
    probability_reduced = low(probs)
    mixed = jnp.einsum('hij,jhd->ihd', probability_reduced, value_head_split, precision=HIGHEST).reshape(SLOT_LEN, D)
    mixed = low(low_back(mixed))
    resid = base + low_back(matmul(mixed, w_out) + b_out)
    normed2 = low(layer_norm(resid, ln2_gain, ln2_shift))
    hidden_pre = low_back(matmul(normed2, w_up) + b_up)
    hidden = low(jax.nn.gelu(hidden_pre, approximate=False))
    atom_out = resid + matmul(hidden, w_down) + b_down
    slot_pen = jnp.sum(jnp.where(pair_mask, logits * logits, 0.0)) / pair_total
    return (atom_out, logits, slot_pen)

def reference(atom_feats, pair_feats, type_ids, mol_lengths, type_table, ln1_gain, ln1_shift, w_query, b_query, w_key, w_value, b_value, w_out, b_out, ln2_gain, ln2_shift, w_up, b_up, w_down, b_down, atom_cotan, pair_cotan):
    pair_total = jnp.sum(mol_lengths * mol_lengths).astype(jnp.float32)
    params = (type_table.astype(jnp.float32), ln1_gain.astype(jnp.float32), ln1_shift.astype(jnp.float32), w_query.astype(jnp.float32), b_query.astype(jnp.float32), w_key.astype(jnp.float32), w_value.astype(jnp.float32), b_value.astype(jnp.float32), w_out.astype(jnp.float32), b_out.astype(jnp.float32), ln2_gain.astype(jnp.float32), ln2_shift.astype(jnp.float32), w_up.astype(jnp.float32), b_up.astype(jnp.float32), w_down.astype(jnp.float32), b_down.astype(jnp.float32))
    checked = jax.checkpoint(slot_layer)

    def forward(weights, atoms_in, pairs_in):

        def one_slot(slot_data):
            atom_slot, pair_slot, type_slot, length_slot = slot_data
            return checked(weights, atom_slot, pair_slot, type_slot, length_slot, pair_total)
        atom_out, pair_out, slot_pen = lax.map(one_slot, (atoms_in, pairs_in, type_ids, mol_lengths))
        return (atom_out, pair_out, jnp.sum(slot_pen))
    primal, pullback = jax.vjp(forward, params, atom_feats.astype(jnp.float32), pair_feats.astype(jnp.float32))
    grads, atoms_back, pairs_back = pullback((atom_cotan.astype(jnp.float32), pair_cotan.astype(jnp.float32), jnp.ones_like(primal[2])))
    return (primal[0].astype(jnp.bfloat16), primal[1].astype(jnp.bfloat16), primal[2].astype(jnp.float32), atoms_back.astype(jnp.bfloat16), pairs_back.astype(jnp.bfloat16), grads[0], grads[1], grads[2], grads[3], grads[4], grads[5], grads[6], grads[7], grads[8], grads[9], grads[10], grads[11], grads[12], grads[13], grads[14], grads[15])
```

```python
import functools

import jax
import jax.numpy as jnp
from jax import lax
from jax.experimental import pallas as pl
from jax.experimental.pallas import tpu as pltpu
from jax.sharding import PartitionSpec as P

EPSILON = 1e-05
HIGHEST = lax.Precision.HIGHEST
F32 = jnp.float32
BF16 = jnp.bfloat16
BIG = 1073741824.0
TN = (((0,), (0,)), ((), ()))
NT = (((1,), (1,)), ((), ()))
NN = (((1,), (0,)), ((), ()))
STEP = 8
PAIR_LIMIT = 6.0
SAFE_LOGIT = 60.0


def dot(left, right, dims):
    return lax.dot_general(left, right, dims, preferred_element_type=F32)


def rounded(values):
    return lax.reduce_precision(values, 8, 7)


def norm_parts(values, gain, shift):
    center = values - jnp.mean(values, axis=-1, keepdims=True)
    inverse = lax.rsqrt(jnp.mean(center * center, axis=-1, keepdims=True) + EPSILON)
    unit_rows = center * inverse
    return (unit_rows * gain + shift, unit_rows, inverse)


def norm_back(upstream, unit_rows, inverse, gain):
    scaled = upstream * gain
    first = jnp.mean(scaled, axis=-1, keepdims=True)
    second = jnp.mean(scaled * unit_rows, axis=-1, keepdims=True)
    grad_in = inverse * (scaled - first - unit_rows * second)
    return (grad_in, jnp.sum(upstream * unit_rows, axis=0), jnp.sum(upstream, axis=0))


def gelu_slope(values):
    cumulative = 0.5 * (1.0 + lax.erf(values * 0.7071067811865476))
    density = jnp.exp(-0.5 * values * values) * 0.3989422804014327
    return cumulative + values * density


def project(left, right):
    return jnp.dot(left, right, preferred_element_type=F32)


def project_back(left, right):
    return jnp.einsum("rd,ed->re", left, right, preferred_element_type=F32)


def weight_grad(left, right):
    return jnp.einsum("rd,re->de", left, right, preferred_element_type=F32)


def forward_body(
    safe, pf, query, key, value, row_ids, col_ids, pair_out, mixed, top, mask, bias, kept
):
    slot = pl.program_id(0)
    group = pl.program_id(1)
    heads = pf.shape[1]

    @pl.when(group == 0)
    def _():
        same = row_ids[0] == col_ids[0]
        mask[...] = jnp.where(same, 1.0, 0.0).astype(BF16)
        bias[...] = jnp.where(same, 0.0, -BIG)

    def logits_of(h):
        logits = dot(query[0, h], key[0, h], TN) + pf[0, h].astype(F32)
        pair_out[0, h] = logits.astype(BF16)
        return logits

    def weigh(h, spot):
        mixed[0, h] = dot(value[0, h], kept[spot], NT)

    is_safe = safe[slot] == 1

    @pl.when(is_safe)
    def _():
        top[...] = jnp.zeros_like(top)

        def block(i, carry):
            for u in range(STEP):
                h = i * STEP + u
                kept[u % 2] = jnp.exp(logits_of(h)).astype(BF16) * mask[...]
                weigh(jnp.maximum(h - 1, 0), (u + 1) % 2)
            return carry

        lax.fori_loop(0, heads // STEP, block, 0)
        weigh(heads - 1, 1)

    @pl.when(jnp.logical_not(is_safe))
    def _():
        def block(i, carry):
            for u in range(STEP):
                h = i * STEP + u
                masked = logits_of(h) + bias[...]
                highest = jnp.max(masked, axis=1, keepdims=True)
                top[0, i, :, u : u + 1] = highest
                kept[0] = jnp.exp(masked - highest).astype(BF16)
                weigh(h, 0)
            return carry

        lax.fori_loop(0, heads // STEP, block, 0)


def attend(safe, pf, query, key, value, row_ids, col_ids, per_step):
    slots, heads, rows, cols = pf.shape

    def by_head(height, width):
        return pl.BlockSpec((1, per_step, height, width), lambda s, g: (s, g, 0, 0))

    return pl.pallas_call(
        forward_body,
        grid=(slots, heads // per_step),
        in_specs=[
            pl.BlockSpec(memory_space=pltpu.SMEM),
            by_head(rows, cols),
            by_head(16, rows),
            by_head(16, cols),
            by_head(16, cols),
            pl.BlockSpec((1, rows, 1), lambda s, g: (s, 0, 0)),
            pl.BlockSpec((1, 1, cols), lambda s, g: (s, 0, 0)),
        ],
        out_specs=[
            by_head(rows, cols),
            by_head(16, rows),
            pl.BlockSpec((1, per_step // STEP, rows, STEP), lambda s, g: (s, g, 0, 0)),
        ],
        out_shape=[
            jax.ShapeDtypeStruct((slots, heads, rows, cols), BF16),
            jax.ShapeDtypeStruct((slots, heads, 16, rows), F32),
            jax.ShapeDtypeStruct((slots, heads // STEP, rows, STEP), F32),
        ],
        scratch_shapes=[
            pltpu.VMEM((rows, cols), BF16),
            pltpu.VMEM((rows, cols), F32),
            pltpu.VMEM((2, rows, cols), BF16),
        ],
        compiler_params=pltpu.CompilerParams(vmem_limit_bytes=56 << 20),
        name="attend",
    )(safe, pf, query, key, value, row_ids, col_ids)


def backward_body(
    scale,
    pf,
    cotan,
    query,
    key,
    grad,
    value,
    query_mask,
    key_mask,
    log_total,
    row_ids,
    col_ids,
    held,
    pair_grad,
    query_grad,
    key_grad,
    value_grad,
    penalty,
    weight,
    probs,
):
    slot = pl.program_id(0)
    group = pl.program_id(1)
    heads = pf.shape[1]
    rows, cols = pf.shape[2:]

    @pl.when(group == 0)
    def _():
        weight[...] = jnp.where(row_ids[0] == col_ids[0], scale[0], 0.0).astype(BF16)

    @pl.when((group == 0) & (slot == 0))
    def _():
        penalty[...] = jnp.zeros_like(penalty)

    def pairs(i, u):
        h = i * STEP + u
        left = jnp.concatenate([query[0, h], query_mask[0]], 0)
        right = jnp.concatenate([key[0, h], key_mask[0]], 0)
        logits = dot(left, right, TN) + pf[0, h].astype(F32)
        probs_grad = dot(grad[0, h], value[0, h], TN).astype(BF16)
        prob = jnp.exp(logits - log_total[0, i, :, u : u + 1]).astype(BF16)
        probs[u % 2] = prob
        logits_low = logits.astype(BF16)
        pen_grad = logits_low * weight[...]
        pair_grad[0, h] = prob * probs_grad + (cotan[0, h] + pen_grad)
        squares = (pen_grad * logits_low).reshape(rows // 64, 4, 16, cols)
        penalty[...] += jnp.sum(jnp.sum(squares, axis=1).astype(F32), axis=0)

    def sums(h, spot):
        upper = dot(query[0, h], pair_grad[0, h], NN)
        key_grad[0, h] = upper[:8] + upper[8:]
        value_grad[0, h] = dot(grad[0, h], probs[spot], NN)[:8]
        query_grad[0, h] = dot(key[0, h], pair_grad[0, h], NT)[:8]

    def block(i, carry):
        for u in range(STEP):
            pairs(i, u)
            sums(jnp.maximum(i * STEP + u - 1, 0), (u + 1) % 2)
        return carry

    lax.fori_loop(0, heads // STEP, block, 0)
    sums(heads - 1, 1)


def attend_back(
    scale,
    pf,
    cotan,
    query,
    key,
    grad,
    value,
    query_mask,
    key_mask,
    log_total,
    row_ids,
    col_ids,
    held,
    first,
    count,
    per_step,
):
    slots, heads, rows, cols = pf.shape
    start = first // per_step

    def by_head(height, width):
        return pl.BlockSpec((1, per_step, height, width), lambda s, g: (s, g + start, 0, 0))

    def part(height, width):
        return pl.BlockSpec((1, per_step, height, width), lambda s, g: (s, g, 0, 0))

    def by_slot(height, width):
        return pl.BlockSpec((1, height, width), lambda s, g: (s, 0, 0))

    operands = [
        scale,
        pf,
        cotan,
        query,
        key,
        grad,
        value,
        query_mask,
        key_mask,
        log_total,
        row_ids,
        col_ids,
    ]
    in_specs = [
        pl.BlockSpec(memory_space=pltpu.SMEM),
        by_head(rows, cols),
        by_head(rows, cols),
        by_head(16, rows),
        by_head(16, cols),
        by_head(16, rows),
        by_head(16, cols),
        by_slot(16, rows),
        by_slot(16, cols),
        pl.BlockSpec((1, per_step // STEP, rows, STEP), lambda s, g: (s, g + start, 0, 0)),
        by_slot(rows, 1),
        by_slot(1, cols),
    ]
    body = backward_body
    aliases = {}
    if held is None:

        def body(*refs):
            backward_body(*refs[:12], None, *refs[12:])

    else:
        operands.append(held)
        in_specs.append(pl.BlockSpec(memory_space=pl.ANY))
        aliases = {12: 0}
    return pl.pallas_call(
        body,
        grid=(slots, count // per_step),
        in_specs=in_specs,
        out_specs=[
            by_head(rows, cols),
            part(8, rows),
            part(8, cols),
            part(8, cols),
            pl.BlockSpec((16, cols), lambda s, g: (0, 0)),
        ],
        out_shape=[
            jax.ShapeDtypeStruct((slots, heads, rows, cols), BF16),
            jax.ShapeDtypeStruct((slots, count, 8, rows), F32),
            jax.ShapeDtypeStruct((slots, count, 8, cols), F32),
            jax.ShapeDtypeStruct((slots, count, 8, cols), F32),
            jax.ShapeDtypeStruct((16, cols), F32),
        ],
        scratch_shapes=[
            pltpu.VMEM((rows, cols), BF16),
            pltpu.VMEM((2, rows, cols), BF16),
        ],
        input_output_aliases=aliases,
        compiler_params=pltpu.CompilerParams(vmem_limit_bytes=56 << 20),
        name="attend_back",
    )(*operands)


def flips(sizes):
    found = []
    for axis in ("slot", "blk"):
        bit = 1
        while bit < sizes[axis]:
            found.append((axis, bit))
            bit *= 2
    return found


def swap(values, sizes, axis, bit):
    return lax.ppermute(values, axis, [(i, i ^ bit) for i in range(sizes[axis])])


def butterfly(values, sizes, axes=("slot", "blk")):
    for axis, bit in flips(sizes):
        if axis in axes:
            values = values + swap(values, sizes, axis, bit)
    return values


def step_plan(sizes):
    whole = sizes["slot"] * sizes["blk"]
    blk = sizes["blk"]
    slot_at = lax.axis_index("slot")
    blk_at = lax.axis_index("blk")

    def partner(device, axis, bit):
        s, b = divmod(device, blk)
        return (s ^ bit) * blk + b if axis == "slot" else s * blk + (b ^ bit)

    def bit_of(axis, bit):
        return ((slot_at if axis == "slot" else blk_at) // bit) % 2

    def plain(axis, bit):
        return ([(d, partner(d, axis, bit)) for d in range(whole)], bit_of(axis, bit))

    def mixed(even, odd):
        pairs = [(d, partner(d, *(even if (d // blk) % 2 == 0 else odd))) for d in range(whole)]
        return (pairs, jnp.where(slot_at % 2 == 0, bit_of(*even), bit_of(*odd)))

    steps = flips(sizes)
    core, rest = steps[0], steps[1:]
    near_y, near_x = ("slot", 2), ("blk", 1)
    plan = [plain(*core)]
    if near_y in rest and near_x in rest:
        rest = [step for step in rest if step not in (near_y, near_x)]
        plan += [mixed(near_x, near_y), mixed(near_y, near_x)]
    return plan + [plain(*step) for step in rest]


def sum_all(values, plan):
    joint = ("slot", "blk")
    for pairs, half in plan:
        halves = values.reshape((2, values.shape[0] // 2) + values.shape[1:])
        away = lax.dynamic_index_in_dim(halves, 1 - half, 0, keepdims=False).astype(BF16)
        mine = lax.dynamic_index_in_dim(halves, half, 0, keepdims=False).astype(F32)
        values = mine + lax.ppermute(away, joint, pairs).astype(F32)
    values = values.astype(BF16)
    for pairs, half in plan[::-1]:
        came = lax.ppermute(values, joint, pairs)
        values = jnp.where(
            half == 0,
            jnp.concatenate([values, came], 0),
            jnp.concatenate([came, values], 0),
        )
    return values.astype(F32)


def local(
    sizes,
    atom_feats,
    pair_feats,
    type_ids,
    mol_lengths,
    type_table,
    ln1_gain,
    ln1_shift,
    w_query,
    b_query,
    w_key,
    w_value,
    b_value,
    w_out,
    b_out,
    ln2_gain,
    ln2_shift,
    w_up,
    b_up,
    w_down,
    b_down,
    atom_cotan,
    pair_cotan,
):
    slots, rows, width = atom_feats.shape
    heads = pair_feats.shape[1]
    cols = pair_feats.shape[3]
    head_size = width // heads
    scale = head_size ** (-0.5)
    flat = slots * rows
    types = type_table.shape[0]
    mols = mol_lengths.shape[1]
    blk_at = lax.axis_index("blk")
    row_start = blk_at * rows
    plan = step_plan(sizes)

    def own(values, axis=1):
        return lax.dynamic_slice_in_dim(values, row_start, rows, axis)

    if sizes["blk"] == 2:

        def gathered(values):
            came = swap(values, sizes, "blk", 1)
            return jnp.where(
                blk_at == 0,
                jnp.concatenate([values, came], 1),
                jnp.concatenate([came, values], 1),
            )

    else:

        def gathered(values):
            return lax.all_gather(values, "blk", axis=1, tiled=True)

    feats = gathered(atom_feats)
    all_types = gathered(type_ids)
    squares = jnp.sum(mol_lengths * mol_lengths).astype(F32)
    pair_total = butterfly(squares.reshape(1, 1), sizes, ("slot",))[0, 0]
    pen_scale = 2.0 / pair_total

    bounds = jnp.cumsum(mol_lengths, axis=1)
    places = jnp.arange(cols, dtype=jnp.int32)
    mol_ids = jnp.sum((places[None, :, None] >= bounds[:, None, :]).astype(jnp.int32), axis=2)
    row_mols = own(mol_ids)
    row_ids = row_mols[:, :, None]
    col_ids = mol_ids[:, None, :]

    def mol_rows(ids):
        return (ids[:, None, :] == jnp.arange(16, dtype=jnp.int32)[None, :, None]).astype(F32)

    query_mask = mol_rows(row_mols).astype(BF16)
    used = (jnp.arange(16) < mols)[None, :, None]
    key_mask = jnp.where(used, -BIG * (1.0 - mol_rows(mol_ids)), 0.0).astype(BF16)

    onehot = (
        all_types.reshape(slots * cols)[:, None] == jnp.arange(types, dtype=jnp.int32)[None, :]
    ).astype(F32)
    base_all = feats.reshape(slots * cols, width).astype(F32) + jnp.dot(
        onehot, type_table, precision=HIGHEST
    )
    normed1, unit1, inverse1 = norm_parts(base_all, ln1_gain, ln1_shift)
    normed1_low = normed1.astype(BF16).reshape(slots, cols, width)
    own_normed1 = own(normed1_low)

    def into_heads(weights, normed):
        turned = jnp.einsum("de,nrd->ner", weights, normed, preferred_element_type=F32)
        return turned

    query = rounded(into_heads(w_query, own_normed1) + b_query[:, None])
    key = rounded(into_heads(w_key, normed1_low)).reshape(slots, heads, head_size, cols)
    value = (into_heads(w_value, normed1_low) + b_value[:, None]).astype(BF16)
    value = value.reshape(slots, heads, head_size, cols)
    query_heads = query.reshape(slots, heads, head_size, rows)
    far_query = jnp.max(jnp.sum(query_heads * query_heads, axis=2), axis=2)
    far_key = jnp.max(jnp.sum(key * key, axis=2), axis=2)
    reach = jnp.max(scale * jnp.sqrt(far_query * far_key), axis=1) + PAIR_LIMIT
    safe = (reach <= SAFE_LOGIT).astype(jnp.int32)
    scaled = query_heads * scale
    upper = rounded(scaled)
    query_rows = jnp.concatenate([upper.astype(BF16), (scaled - upper).astype(BF16)], 2)
    key_low = key.astype(BF16)
    key_rows = jnp.concatenate([key_low, key_low], 2)
    value_rows = jnp.concatenate(
        [
            value,
            jnp.ones((slots, heads, 3, cols), BF16),
            jnp.zeros((slots, heads, 5, cols), BF16),
        ],
        2,
    )

    pair_out, weighed, top = attend(
        safe, pair_feats, query_rows, key_rows, value_rows, row_ids, col_ids, 8
    )
    totals = weighed[:, :, 8]
    mixed_turned = weighed[:, :, :8] / totals[:, :, None]
    mixed_low = (
        jnp.swapaxes(mixed_turned.reshape(slots, width, rows), 1, 2)
        .reshape(flat, width)
        .astype(BF16)
    )
    log_total = top + jnp.swapaxes(
        jnp.log(totals).reshape(slots, heads // STEP, STEP, rows), 2, 3
    )

    base = own(base_all.reshape(slots, cols, width)).reshape(flat, width)
    resid = base + project(mixed_low, w_out) + b_out
    normed2, unit2, inverse2 = norm_parts(resid, ln2_gain, ln2_shift)
    normed2_low = normed2.astype(BF16)
    hidden_pre = project(normed2_low, w_up) + b_up
    hidden_low = jax.nn.gelu(hidden_pre, approximate=False).astype(BF16)
    atom_out = resid + project(hidden_low, w_down) + b_down
    out_grad = atom_cotan.reshape(flat, width)
    g_w_down = weight_grad(hidden_low, out_grad)
    g_b_down = jnp.sum(out_grad.astype(F32), axis=0)
    hidden_grad = project_back(out_grad, w_down) * gelu_slope(hidden_pre)
    hidden_grad_low = hidden_grad.astype(BF16)
    g_w_up = weight_grad(normed2_low, hidden_grad_low)
    g_b_up = jnp.sum(hidden_grad_low.astype(F32), axis=0)
    resid_back, g_ln2_gain, g_ln2_shift = norm_back(
        project_back(hidden_grad_low, w_up), unit2, inverse2, ln2_gain
    )
    resid_grad = out_grad.astype(F32) + resid_back
    resid_grad_low = resid_grad.astype(BF16)
    g_w_out = weight_grad(mixed_low, resid_grad_low)
    g_b_out = jnp.sum(resid_grad_low.astype(F32), axis=0)
    g_w_down, g_w_up, g_w_out = (sum_all(g, plan) for g in (g_w_down, g_w_up, g_w_out))

    mixed_grad = rounded(
        jnp.einsum(
            "de,nre->ndr",
            w_out,
            resid_grad_low.reshape(slots, rows, width),
            preferred_element_type=F32,
        )
    ).reshape(slots, heads, head_size, rows)
    delta = -jnp.sum(mixed_grad * mixed_turned, axis=2)
    first = rounded(delta)
    second = rounded(delta - first)
    third = delta - first - second
    grad_rows = jnp.concatenate(
        [
            mixed_grad.astype(BF16),
            jnp.stack([first, second, third], 2).astype(BF16),
            jnp.zeros((slots, heads, 5, rows), BF16),
        ],
        2,
    )

    pair_grad, query_part, key_part, value_part, pen_tile = attend_back(
        pen_scale.reshape(1),
        pair_feats,
        pair_cotan,
        query_rows,
        key_rows,
        grad_rows,
        value_rows,
        query_mask,
        key_mask,
        log_total,
        row_ids,
        col_ids,
        None,
        0,
        heads,
        8,
    )
    penalty = 0.5 * jnp.sum(pen_tile)

    query_grad = (query_part * scale).astype(BF16).reshape(slots, width, rows)
    key_grad = key_part.astype(BF16).reshape(slots, width, cols)
    value_grad = value_part.astype(BF16).reshape(slots, width, cols)

    def turned_grad(normed, grads):
        return jnp.einsum("nrd,ner->de", normed, grads, preferred_element_type=F32)

    g_w_query = turned_grad(own_normed1, query_grad)
    g_w_key = turned_grad(normed1_low, key_grad)
    g_w_value = turned_grad(normed1_low, value_grad)
    g_b_query = jnp.sum(query_grad.astype(F32), axis=(0, 2))
    g_b_value = jnp.sum(value_part, axis=(0, 3)).reshape(width)
    g_w_query, g_w_key, g_w_value = (sum_all(g, plan) for g in (g_w_query, g_w_key, g_w_value))

    def turned_back(weights, grads):
        return jnp.einsum("de,ner->nrd", weights, grads, preferred_element_type=F32)

    norm_in = turned_back(w_key, key_grad) + turned_back(w_value, value_grad)
    query_in = turned_back(w_query, query_grad)
    norm_in = lax.dynamic_update_slice_in_dim(norm_in, own(norm_in) + query_in, row_start, 1)
    base_back, g_ln1_gain, g_ln1_shift = norm_back(
        norm_in.reshape(slots * cols, width), unit1, inverse1, ln1_gain
    )
    back_parts = base_back.reshape(slots, cols, width)
    resid_rows = resid_grad.reshape(slots, rows, width)
    table_rows = lax.dynamic_update_slice_in_dim(
        back_parts, own(back_parts) + resid_rows, row_start, 1
    )
    g_type_table = jnp.einsum(
        "rt,rd->td", onehot, table_rows.reshape(slots * cols, width), precision=HIGHEST
    )
    if sizes["blk"] == 2:
        away = lax.dynamic_slice_in_dim(back_parts, (1 - blk_at) * rows, rows, 1).astype(BF16)
        base_grad = own(back_parts) + swap(away, sizes, "blk", 1).astype(F32) + resid_rows
    else:
        base_grad = resid_rows + lax.psum_scatter(
            back_parts, "blk", scatter_dimension=1, tiled=True
        )

    small = [
        g_type_table,
        g_ln1_gain,
        g_ln1_shift,
        g_b_query,
        g_b_value,
        g_b_out,
        g_ln2_gain,
        g_ln2_shift,
        g_b_up,
        g_b_down,
    ]
    packed = jnp.concatenate(
        [g.reshape(-1, width) for g in small] + [jnp.full((1, width), penalty)], 0
    )
    packed = butterfly(packed, sizes)
    spread = []
    at = 0
    for g in small:
        high = g.size // width
        spread.append(packed[at : at + high].reshape(g.shape))
        at += high
    penalty = packed[at, 0]
    (
        g_type_table,
        g_ln1_gain,
        g_ln1_shift,
        g_b_query,
        g_b_value,
        g_b_out,
        g_ln2_gain,
        g_ln2_shift,
        g_b_up,
        g_b_down,
    ) = spread
    return (
        atom_out.reshape(slots, rows, width).astype(BF16),
        pair_out,
        penalty,
        base_grad.astype(BF16),
        pair_grad,
        g_type_table,
        g_ln1_gain,
        g_ln1_shift,
        g_w_query,
        g_b_query,
        g_w_key,
        g_w_value,
        g_b_value,
        g_w_out,
        g_b_out,
        g_ln2_gain,
        g_ln2_shift,
        g_w_up,
        g_b_up,
        g_w_down,
        g_b_down,
    )


def solution(mesh):
    atoms = P("slot", "blk", None)
    pairs = P("slot", None, "blk", None)
    sizes = {axis: mesh.shape[axis] for axis in ("slot", "blk")}
    return jax.shard_map(
        functools.partial(local, sizes),
        mesh=mesh,
        in_specs=(atoms, pairs, P("slot", "blk"), P("slot", None))
        + (P(),) * 16
        + (atoms, pairs),
        out_specs=(atoms, pairs, P(), atoms, pairs) + (P(),) * 16,
        check_vma=False,
    )
```

```python
import functools

import jax
import jax.numpy as jnp
from jax import lax
from jax.experimental import pallas as pl
from jax.experimental.pallas import tpu as pltpu
from jax.sharding import PartitionSpec as P

EPSILON = 1e-05
F32 = jnp.float32
BF16 = jnp.bfloat16
BIG = 1073741824.0
TN = (((0,), (0,)), ((), ()))
NT = (((1,), (1,)), ((), ()))
NN = (((1,), (0,)), ((), ()))
TT = (((0,), (1,)), ((), ()))
STEP = 8
CHUNK = 512
PAIR_LIMIT = 6.0
SAFE_LOGIT = 40.0


def dot(left, right, dims):
    return lax.dot_general(left, right, dims, preferred_element_type=F32)


def rounded(values):
    return lax.reduce_precision(values, 8, 7)


def unit_of(values):
    center = values - jnp.mean(values, axis=-1, keepdims=True)
    inverse = lax.rsqrt(jnp.mean(center * center, axis=-1, keepdims=True) + EPSILON)
    return center * inverse, inverse


def norm_back(upstream, unit, inverse, gain):
    scaled = upstream * gain
    first = jnp.mean(scaled, axis=-1, keepdims=True)
    second = jnp.mean(scaled * unit, axis=-1, keepdims=True)
    return inverse * (scaled - first - unit * second)


def column_sum(values):
    return jnp.sum(values, axis=0, keepdims=True)


def onehot_of(ids, types, copies):
    lane = lax.broadcasted_iota(jnp.int32, (ids.shape[0], types * copies), 1)
    hit = lane == ids
    for i in range(1, copies):
        hit = hit | (lane == ids + i * types)
    return jnp.where(hit, 1.0, 0.0).astype(BF16)


def whole(shape):
    return pl.BlockSpec(shape, lambda *grid: (0,) * len(shape))


def by_slot(*shape):
    return pl.BlockSpec((1,) + shape, lambda s: (s,) + (0,) * len(shape))


def prepare_body(
    start,
    feats,
    types,
    table,
    gain,
    shift,
    w_query,
    b_query,
    w_key,
    w_value,
    b_value,
    base_out,
    normed_out,
    query_out,
    key_out,
    value_out,
    reach,
):
    heads, _, rows = query_out.shape[1:]
    cols, width = feats.shape[1:]
    size = width // heads
    base = feats[0].astype(F32) + dot(
        onehot_of(types[0], table.shape[0] // 3, 3), table[...], NN
    )
    base_out[0] = base
    unit, _ = unit_of(base)
    normed = (unit * gain[...] + shift[...]).astype(BF16)
    normed_out[0] = normed

    def split_heads(values):
        return values.reshape(heads, size, values.shape[1])

    def far(values):
        return jnp.max(jnp.sum(values * values, axis=1), axis=1, keepdims=True)

    key = split_heads(dot(w_key[...], normed, TT).astype(BF16).astype(F32))
    key_out[0] = jnp.concatenate([key, key], 1).astype(BF16)
    value = split_heads(dot(w_value[...], normed, TT) + b_value[...])
    line = lax.broadcasted_iota(jnp.int32, (heads, size, cols), 1)
    value_out[0] = jnp.concatenate([value, jnp.where(line < 3, 1.0, 0.0)], 1).astype(BF16)
    own = normed_out[0, pl.ds(pl.multiple_of(start[0], rows), rows), :]
    query = split_heads((dot(w_query[...], own, TT) + b_query[...]).astype(BF16).astype(F32))
    scaled = query * size ** (-0.5)
    upper = scaled.astype(BF16).astype(F32)
    query_out[0] = jnp.concatenate([upper, scaled - upper], 1).astype(BF16)
    reach[0] = jnp.broadcast_to(jnp.max(far(query) * far(key)), reach.shape[1:])


def prepare(start, feats, types, table, gain, shift, w_query, b_query, w_key, w_value, b_value, heads, rows):
    slots, cols, width = feats.shape
    square = whole((width, width))
    row, column = whole((1, width)), whole((width, 1))
    shapes = [
        ((cols, width), F32),
        ((cols, width), BF16),
        ((heads, 16, rows), BF16),
        ((heads, 16, cols), BF16),
        ((heads, 16, cols), BF16),
        ((8, 128), F32),
    ]
    return pl.pallas_call(
        prepare_body,
        grid=(slots,),
        in_specs=[
            pl.BlockSpec(memory_space=pltpu.SMEM),
            by_slot(cols, width),
            by_slot(cols, 1),
            whole(table.shape),
            row,
            row,
            square,
            column,
            square,
            square,
            column,
        ],
        out_specs=[by_slot(*shape) for shape, _ in shapes],
        out_shape=[jax.ShapeDtypeStruct((slots,) + shape, kind) for shape, kind in shapes],
        compiler_params=pltpu.CompilerParams(vmem_limit_bytes=56 << 20),
        name="prepare",
    )(start, feats, types, table, gain, shift, w_query, b_query, w_key, w_value, b_value)


def feed_body(
    weighed,
    top,
    base,
    cotan,
    w_out,
    b_out,
    gain,
    shift,
    w_up,
    b_up,
    w_down,
    b_down,
    atom_out,
    grad_rows,
    log_total,
    resid_grad_out,
    g_weights,
    g_b_up,
    g_rows,
    total,
):
    slot = pl.program_id(0)
    heads, _, rows = weighed.shape[1:]
    width = base.shape[2]
    size = width // heads
    hidden_width = w_up.shape[1]

    @pl.when(slot == 0)
    def _():
        for ref in (total, g_b_up, g_rows):
            ref[...] = jnp.zeros_like(ref)

    totals = weighed[0, :, size : size + 1, :]
    mixed = weighed[0, :, :size, :] / totals
    logs = jnp.log(totals).reshape(heads, rows)
    for g in range(heads // STEP):
        log_total[0, g] = top[0, g] + logs[g * STEP : (g + 1) * STEP].T
    mixed_low = mixed.reshape(width, rows).astype(BF16)
    resid = base[0] + dot(mixed_low, w_out[...], TN) + b_out[...]
    unit, inverse = unit_of(resid)
    normed = (unit * gain[...] + shift[...]).astype(BF16)
    grad = cotan[0]
    down = jnp.zeros((rows, width), F32)
    back = jnp.zeros((rows, width), F32)
    for at in range(0, hidden_width, CHUNK):
        part = slice(at, at + CHUNK)
        pre = dot(normed, w_up[:, part], NN) + b_up[:, part]
        cumulative = 0.5 * (1.0 + lax.erf(pre * 0.7071067811865476))
        density = jnp.exp(-0.5 * pre * pre) * 0.3989422804014327
        hidden = (pre * cumulative).astype(BF16)
        down += dot(hidden, w_down[part, :], NN)
        total[part, :] += dot(hidden, grad, TN)
        hidden_grad = (
            dot(grad, w_down[part, :], NT) * (cumulative + pre * density)
        ).astype(BF16)
        back += dot(hidden_grad, w_up[:, part], NT)
        total[hidden_width + width + at : hidden_width + 2 * width + at] += dot(
            normed, hidden_grad, TN
        )
        g_b_up[:, part] += column_sum(hidden_grad.astype(F32))
    atom_out[0] = (resid + down + b_down[...]).astype(BF16)
    resid_grad = grad.astype(F32) + norm_back(back, unit, inverse, gain[...])
    resid_grad_out[0] = resid_grad
    low = resid_grad.astype(BF16)
    total[hidden_width : hidden_width + width] += dot(mixed_low, low, NN)
    g_rows[0:1] += column_sum(low.astype(F32))
    g_rows[1:2] += column_sum(back * unit)
    g_rows[2:3] += column_sum(back)
    g_rows[3:4] += column_sum(grad.astype(F32))
    mixed_grad = dot(w_out[...], low, NT).astype(BF16).astype(F32).reshape(heads, size, rows)
    delta = -jnp.sum(mixed_grad * mixed, axis=1, keepdims=True)
    first = delta.astype(BF16).astype(F32)
    second = (delta - first).astype(BF16).astype(F32)
    line = lax.broadcasted_iota(jnp.int32, (heads, size, rows), 1)
    extra = jnp.where(
        line == 0,
        first,
        jnp.where(line == 1, second, jnp.where(line == 2, delta - first - second, 0.0)),
    )
    grad_rows[0] = jnp.concatenate([mixed_grad, extra], 1).astype(BF16)

    @pl.when(slot == pl.num_programs(0) - 1)
    def _():
        g_weights[...] = total[...].astype(BF16)


def feed(weighed, top, base, cotan, w_out, b_out, gain, shift, w_up, b_up, w_down, b_down):
    slots, heads, _, rows = weighed.shape
    width, hidden = w_up.shape
    row = whole((1, width))
    own = [
        ((rows, width), BF16),
        ((heads, 16, rows), BF16),
        ((heads // STEP, rows, STEP), F32),
        ((rows, width), F32),
    ]
    shared = [
        ((2 * hidden + width, width), BF16),
        ((1, hidden), F32),
        ((4, width), F32),
    ]
    return pl.pallas_call(
        feed_body,
        grid=(slots,),
        in_specs=[
            by_slot(heads, 16, rows),
            by_slot(heads // STEP, rows, STEP),
            by_slot(rows, width),
            by_slot(rows, width),
            whole((width, width)),
            row,
            row,
            row,
            whole((width, hidden)),
            whole((1, hidden)),
            whole((hidden, width)),
            row,
        ],
        out_specs=[by_slot(*shape) for shape, _ in own] + [whole(shape) for shape, _ in shared],
        out_shape=[jax.ShapeDtypeStruct((slots,) + shape, kind) for shape, kind in own]
        + [jax.ShapeDtypeStruct(shape, kind) for shape, kind in shared],
        scratch_shapes=[pltpu.VMEM(shared[0][0], F32)],
        compiler_params=pltpu.CompilerParams(vmem_limit_bytes=60 << 20),
        name="feed",
    )(weighed, top, base, cotan, w_out, b_out, gain, shift, w_up, b_up, w_down, b_down)


def finish_body(
    start,
    query_part,
    key_part,
    value_part,
    base,
    normed,
    types,
    resid_grad,
    gain,
    w_query,
    w_key,
    w_value,
    back_out,
    g_weights,
    g_table,
    g_rows,
    g_columns,
    g_turned,
    upstream,
):
    slot = pl.program_id(0)
    rows, width = resid_grad.shape[1:]
    cols = base.shape[1]
    heads, size = query_part.shape[1:3]
    own = pl.ds(pl.multiple_of(start[0], rows), rows)

    @pl.when(slot == 0)
    def _():
        for ref in (g_turned, g_table, g_rows, g_columns):
            ref[...] = jnp.zeros_like(ref)

    query_wide = (query_part[0] * size ** (-0.5)).reshape(width, rows)
    value_wide = value_part[0].reshape(width, cols)
    query_grad = query_wide.astype(BF16)
    key_grad = key_part[0].reshape(width, cols).astype(BF16)
    value_grad = value_wide.astype(BF16)
    g_turned[0] += dot(query_grad, normed[0, own, :], NN)
    g_turned[1] += dot(key_grad, normed[0], NN)
    g_turned[2] += dot(value_grad, normed[0], NN)
    g_columns[0] += jnp.sum(query_grad.astype(F32), axis=1, keepdims=True)
    g_columns[1] += jnp.sum(value_wide, axis=1, keepdims=True)
    upstream[...] = dot(key_grad, w_key[...], TT) + dot(value_grad, w_value[...], TT)
    upstream[own, :] += dot(query_grad, w_query[...], TT)
    unit, inverse = unit_of(base[0])
    received = upstream[...]
    g_rows[0:1] += column_sum(received * unit)
    g_rows[1:2] += column_sum(received)
    upstream[...] = norm_back(received, unit, inverse, gain[...])
    back_out[0] = upstream[...]
    upstream[own, :] += resid_grad[0]
    total = upstream[...]
    upper = total.astype(BF16)
    lower = (total - upper.astype(F32)).astype(BF16)
    onehot = onehot_of(types[0], g_table.shape[0], 1)
    g_table[...] += dot(onehot, upper, TN) + dot(onehot, lower, TN)

    @pl.when(slot == pl.num_programs(0) - 1)
    def _():
        for i in range(3):
            g_weights[i * width : (i + 1) * width] = g_turned[i].T


def finish(
    start,
    query_part,
    key_part,
    value_part,
    base,
    normed,
    types,
    resid_grad,
    gain,
    w_query,
    w_key,
    w_value,
    type_count,
):
    slots, heads, size, rows = query_part.shape
    cols, width = base.shape[1:]
    square = whole((width, width))
    shared = [
        ((3 * width, width), F32),
        ((type_count, width), F32),
        ((2, width), F32),
        ((2, width, 1), F32),
    ]
    return pl.pallas_call(
        finish_body,
        grid=(slots,),
        in_specs=[
            pl.BlockSpec(memory_space=pltpu.SMEM),
            by_slot(heads, size, rows),
            by_slot(heads, size, cols),
            by_slot(heads, size, cols),
            by_slot(cols, width),
            by_slot(cols, width),
            by_slot(cols, 1),
            by_slot(rows, width),
            whole((1, width)),
            square,
            square,
            square,
        ],
        out_specs=[by_slot(cols, width)] + [whole(shape) for shape, _ in shared],
        out_shape=[jax.ShapeDtypeStruct((slots, cols, width), F32)]
        + [jax.ShapeDtypeStruct(shape, kind) for shape, kind in shared],
        scratch_shapes=[pltpu.VMEM((3, width, width), F32), pltpu.VMEM((cols, width), F32)],
        compiler_params=pltpu.CompilerParams(vmem_limit_bytes=56 << 20),
        name="finish",
    )(
        start,
        query_part,
        key_part,
        value_part,
        base,
        normed,
        types,
        resid_grad,
        gain,
        w_query,
        w_key,
        w_value,
    )


def forward_body(
    safe, pf, query, key, value, row_ids, col_ids, mixed, top, mask, bias, kept
):
    slot = pl.program_id(0)
    group = pl.program_id(1)
    heads = pf.shape[1]

    @pl.when(group == 0)
    def _():
        same = row_ids[0] == col_ids[0]
        mask[...] = jnp.where(same, 1.0, 0.0).astype(BF16)
        bias[...] = jnp.where(same, 0.0, -BIG)

    def logits_of(h):
        return dot(query[0, h], key[0, h], TN) + pf[0, h].astype(F32)

    def weigh(h, spot):
        mixed[0, h] = dot(value[0, h], kept[spot], NT)

    is_safe = safe[slot] == 1

    @pl.when(is_safe)
    def _():
        top[...] = jnp.zeros_like(top)

        for h in range(heads):
            kept[h % 2] = jnp.exp(logits_of(h)).astype(BF16) * mask[...]
            if h:
                weigh(h - 1, (h - 1) % 2)
        weigh(heads - 1, (heads - 1) % 2)

    @pl.when(jnp.logical_not(is_safe))
    def _():
        def block(i, carry):
            for u in range(STEP):
                h = i * STEP + u
                masked = logits_of(h) + bias[...]
                highest = jnp.max(masked, axis=1, keepdims=True)
                top[0, i, :, u : u + 1] = highest
                kept[0] = jnp.exp(masked - highest).astype(BF16)
                weigh(h, 0)
            return carry

        lax.fori_loop(0, heads // STEP, block, 0)


def attend(safe, pf, query, key, value, row_ids, col_ids, per_step):
    slots, heads, rows, cols = pf.shape

    def by_head(height, width):
        return pl.BlockSpec((1, per_step, height, width), lambda s, g: (s, g, 0, 0))

    return pl.pallas_call(
        forward_body,
        grid=(slots, heads // per_step),
        in_specs=[
            pl.BlockSpec(memory_space=pltpu.SMEM),
            by_head(rows, cols),
            by_head(16, rows),
            by_head(16, cols),
            by_head(16, cols),
            pl.BlockSpec((1, rows, 1), lambda s, g: (s, 0, 0)),
            pl.BlockSpec((1, 1, cols), lambda s, g: (s, 0, 0)),
        ],
        out_specs=[
            by_head(16, rows),
            pl.BlockSpec((1, per_step // STEP, rows, STEP), lambda s, g: (s, g, 0, 0)),
        ],
        out_shape=[
            jax.ShapeDtypeStruct((slots, heads, 16, rows), F32),
            jax.ShapeDtypeStruct((slots, heads // STEP, rows, STEP), F32),
        ],
        scratch_shapes=[
            pltpu.VMEM((rows, cols), BF16),
            pltpu.VMEM((rows, cols), F32),
            pltpu.VMEM((2, rows, cols), BF16),
        ],
        compiler_params=pltpu.CompilerParams(vmem_limit_bytes=56 << 20),
        name="attend",
    )(safe, pf, query, key, value, row_ids, col_ids)


def backward_body(
    safe,
    scale,
    pf,
    cotan,
    query,
    key,
    grad,
    value,
    log_total,
    row_ids,
    col_ids,
    pair_out,
    pair_grad,
    query_grad,
    key_grad,
    value_grad,
    penalty,
    weight,
    mask,
    bias,
    probs,
):
    slot = pl.program_id(0)
    group = pl.program_id(1)
    heads = pf.shape[1]
    rows, cols = pf.shape[2:]

    @pl.when(group == 0)
    def _():
        same = row_ids[0] == col_ids[0]
        weight[...] = jnp.where(same, scale[0], 0.0).astype(BF16)
        mask[...] = jnp.where(same, 1.0, 0.0).astype(BF16)
        bias[...] = jnp.where(same, 0.0, -BIG)

    @pl.when((group == 0) & (slot == 0))
    def _():
        penalty[...] = jnp.zeros_like(penalty)

    def pairs(i, u, safe):
        h = i * STEP + u
        logits = dot(query[0, h], key[0, h], TN) + pf[0, h].astype(F32)
        logits_low = logits.astype(BF16)
        pair_out[0, h] = logits_low
        probs_grad = dot(grad[0, h], value[0, h], TN).astype(BF16)
        shifted = logits - log_total[0, i, :, u : u + 1]
        if safe:
            prob = jnp.exp(shifted).astype(BF16) * mask[...]
        else:
            prob = jnp.exp(shifted + bias[...]).astype(BF16)
        probs[h % 2] = prob
        pen_grad = logits_low * weight[...]
        pair_grad[0, h] = prob * probs_grad + (cotan[0, h] + pen_grad)
        squares = pen_grad * logits_low
        while squares.shape[0] > 16:
            half = squares.shape[0] // 2
            squares = squares[:half] + squares[half:]
        penalty[...] += squares.astype(F32)

    def sums(h, spot):
        upper = dot(query[0, h], pair_grad[0, h], NN)
        key_grad[0, h] = upper[:8] + upper[8:]
        value_grad[0, h] = dot(grad[0, h], probs[spot], NN)[:8]
        query_grad[0, h] = dot(key[0, h], pair_grad[0, h], NT)[:8]

    is_safe = safe[slot] == 1

    @pl.when(is_safe)
    def _():
        for h in range(heads):
            pairs(h // STEP, h % STEP, True)
            if h:
                sums(h - 1, (h - 1) % 2)
        sums(heads - 1, (heads - 1) % 2)

    @pl.when(jnp.logical_not(is_safe))
    def _():
        for h in range(heads):
            pairs(h // STEP, h % STEP, False)
            sums(h, h % 2)


def attend_back(
    safe, scale, pf, cotan, query, key, grad, value, log_total, row_ids, col_ids, per_step
):
    slots, heads, rows, cols = pf.shape

    def by_head(height, width):
        return pl.BlockSpec((1, per_step, height, width), lambda s, g: (s, g, 0, 0))

    return pl.pallas_call(
        backward_body,
        grid=(slots, heads // per_step),
        in_specs=[
            pl.BlockSpec(memory_space=pltpu.SMEM),
            pl.BlockSpec(memory_space=pltpu.SMEM),
            by_head(rows, cols),
            by_head(rows, cols),
            by_head(16, rows),
            by_head(16, cols),
            by_head(16, rows),
            by_head(16, cols),
            pl.BlockSpec((1, per_step // STEP, rows, STEP), lambda s, g: (s, g, 0, 0)),
            pl.BlockSpec((1, rows, 1), lambda s, g: (s, 0, 0)),
            pl.BlockSpec((1, 1, cols), lambda s, g: (s, 0, 0)),
        ],
        out_specs=[
            by_head(rows, cols),
            by_head(rows, cols),
            by_head(8, rows),
            by_head(8, cols),
            by_head(8, cols),
            pl.BlockSpec((16, cols), lambda s, g: (0, 0)),
        ],
        out_shape=[
            jax.ShapeDtypeStruct((slots, heads, rows, cols), BF16),
            jax.ShapeDtypeStruct((slots, heads, rows, cols), BF16),
            jax.ShapeDtypeStruct((slots, heads, 8, rows), F32),
            jax.ShapeDtypeStruct((slots, heads, 8, cols), F32),
            jax.ShapeDtypeStruct((slots, heads, 8, cols), F32),
            jax.ShapeDtypeStruct((16, cols), F32),
        ],
        scratch_shapes=[
            pltpu.VMEM((rows, cols), BF16),
            pltpu.VMEM((rows, cols), BF16),
            pltpu.VMEM((rows, cols), F32),
            pltpu.VMEM((2, rows, cols), BF16),
        ],
        compiler_params=pltpu.CompilerParams(vmem_limit_bytes=60 << 20),
        name="attend_back",
    )(safe, scale, pf, cotan, query, key, grad, value, log_total, row_ids, col_ids)


def flips(sizes):
    found = []
    for axis in ("slot", "blk"):
        bit = 1
        while bit < sizes[axis]:
            found.append((axis, bit))
            bit *= 2
    return found


def swap(values, sizes, axis, bit):
    return lax.ppermute(values, axis, [(i, i ^ bit) for i in range(sizes[axis])])


def butterfly(values, sizes, axes=("slot", "blk")):
    for axis, bit in flips(sizes):
        if axis in axes:
            values = values + swap(values, sizes, axis, bit)
    return values


def step_plan(sizes):
    whole = sizes["slot"] * sizes["blk"]
    blk = sizes["blk"]
    slot_at = lax.axis_index("slot")
    blk_at = lax.axis_index("blk")

    def partner(device, axis, bit):
        s, b = divmod(device, blk)
        return (s ^ bit) * blk + b if axis == "slot" else s * blk + (b ^ bit)

    def bit_of(axis, bit):
        return ((slot_at if axis == "slot" else blk_at) // bit) % 2

    def plain(axis, bit):
        return ([(d, partner(d, axis, bit)) for d in range(whole)], bit_of(axis, bit))

    def mixed(even, odd):
        pairs = [(d, partner(d, *(even if (d // blk) % 2 == 0 else odd))) for d in range(whole)]
        return (pairs, jnp.where(slot_at % 2 == 0, bit_of(*even), bit_of(*odd)))

    steps = flips(sizes)
    core, rest = steps[0], steps[1:]
    near_y, near_x = ("slot", 2), ("blk", 1)
    plan = [plain(*core)]
    if near_y in rest and near_x in rest:
        rest = [step for step in rest if step not in (near_y, near_x)]
        plan += [mixed(near_x, near_y), mixed(near_y, near_x)]
    return plan + [plain(*step) for step in rest]


def sum_all(wide, small, plan):
    joint = ("slot", "blk")
    rows, extra = wide.shape[1], small.shape[1]

    def parcel(wide, small):
        upper = rounded(small)
        parts = [wide.astype(BF16), upper.astype(BF16), (small - upper).astype(BF16)]
        return jnp.concatenate(parts, 1)

    def unpack(values):
        values = values.astype(F32)
        return values[:, :rows], values[:, rows : rows + extra] + values[:, rows + extra :]

    def pick(values, half):
        halves = values.reshape((2, values.shape[0] // 2) + values.shape[1:])
        return lax.dynamic_index_in_dim(halves, half, 0, keepdims=False)

    for pairs, half in plan:
        away = parcel(pick(wide, 1 - half), pick(small, 1 - half))
        came_wide, came_small = unpack(lax.ppermute(away, joint, pairs))
        wide = pick(wide, half) + came_wide
        small = pick(small, half) + came_small
    values = parcel(wide, small)
    for pairs, half in plan[::-1]:
        came = lax.ppermute(values, joint, pairs)
        values = jnp.where(
            half == 0,
            jnp.concatenate([values, came], 0),
            jnp.concatenate([came, values], 0),
        )
    return unpack(values)


def sum_wide(values, sizes):
    joint = ("slot", "blk")
    count = sizes["slot"] * sizes["blk"]
    terms = lax.all_to_all(values, joint, 0, 0, tiled=True)
    terms = terms.reshape((count, values.shape[0] // count, values.shape[1]))
    return lax.all_gather(jnp.sum(terms.astype(F32), axis=0).astype(BF16), joint, tiled=True)


def local(
    sizes,
    atom_feats,
    pair_feats,
    type_ids,
    mol_lengths,
    type_table,
    ln1_gain,
    ln1_shift,
    w_query,
    b_query,
    w_key,
    w_value,
    b_value,
    w_out,
    b_out,
    ln2_gain,
    ln2_shift,
    w_up,
    b_up,
    w_down,
    b_down,
    atom_cotan,
    pair_cotan,
):
    slots, rows, width = atom_feats.shape
    heads = pair_feats.shape[1]
    cols = pair_feats.shape[3]
    types = type_table.shape[0]
    blk_at = lax.axis_index("blk")
    row_start = blk_at * rows
    plan = step_plan(sizes)

    def own(values, axis=1):
        return lax.dynamic_slice_in_dim(values, row_start, rows, axis)

    if sizes["blk"] == 2:

        def gathered(values):
            came = swap(values, sizes, "blk", 1)
            return jnp.where(
                blk_at == 0,
                jnp.concatenate([values, came], 1),
                jnp.concatenate([came, values], 1),
            )

    else:

        def gathered(values):
            return lax.all_gather(values, "blk", axis=1, tiled=True)

    feats = gathered(atom_feats)
    all_types = gathered(type_ids)
    squares = jnp.sum(mol_lengths * mol_lengths).astype(F32)
    pair_total = butterfly(squares.reshape(1, 1), sizes, ("slot",))[0, 0]
    pen_scale = 2.0 / pair_total
    feats, pen_scale = lax.optimization_barrier((feats, pen_scale))

    bounds = jnp.cumsum(mol_lengths, axis=1)
    places = jnp.arange(cols, dtype=jnp.int32)
    mol_ids = jnp.sum((places[None, :, None] >= bounds[:, None, :]).astype(jnp.int32), axis=2)
    row_mols = own(mol_ids)
    row_ids = row_mols[:, :, None]
    col_ids = mol_ids[:, None, :]

    first = rounded(type_table)
    second = rounded(type_table - first)
    table = jnp.concatenate([first, second, type_table - first - second], 0).astype(BF16)
    types_column = all_types[:, :, None]
    start = row_start.astype(jnp.int32).reshape(1)

    def line(values):
        return values.reshape(1, -1)

    def column(values):
        return values.reshape(-1, 1)

    base, normed, query_rows, key_rows, value_rows, reach = prepare(
        start,
        feats,
        types_column,
        table,
        line(ln1_gain),
        line(ln1_shift),
        w_query,
        column(b_query),
        w_key,
        w_value,
        column(b_value),
        heads,
        rows,
    )
    furthest = (width // heads) ** (-0.5) * jnp.sqrt(reach[:, 0, 0]) + PAIR_LIMIT
    safe = (furthest <= SAFE_LOGIT).astype(jnp.int32)

    weighed, top = attend(
        safe, pair_feats, query_rows, key_rows, value_rows, row_ids, col_ids, 16
    )
    atom_out, grad_rows, log_total, resid_grad, g_feed, g_b_up, feed_rows = feed(
        weighed,
        top,
        own(base),
        atom_cotan,
        w_out,
        line(b_out),
        line(ln2_gain),
        line(ln2_shift),
        w_up,
        line(b_up),
        w_down,
        line(b_down),
    )
    g_feed = sum_wide(g_feed, sizes)

    pair_out, pair_grad, query_part, key_part, value_part, pen_tile = attend_back(
        safe,
        pen_scale.reshape(1),
        pair_feats,
        pair_cotan,
        query_rows,
        key_rows,
        grad_rows,
        value_rows,
        log_total,
        row_ids,
        col_ids,
        16,
    )
    penalty = 0.5 * jnp.sum(pen_tile)

    back, g_weights, g_type_table, norm_rows, bias_columns = finish(
        start,
        query_part,
        key_part,
        value_part,
        base,
        normed,
        types_column,
        resid_grad,
        line(ln1_gain),
        w_query,
        w_key,
        w_value,
        types,
    )
    if sizes["blk"] == 2:
        away = lax.dynamic_slice_in_dim(back, (1 - blk_at) * rows, rows, 1).astype(BF16)
        base_grad = own(back) + swap(away, sizes, "blk", 1).astype(F32) + resid_grad
    else:
        base_grad = resid_grad + lax.psum_scatter(back, "blk", scatter_dimension=1, tiled=True)
    parts = [g_type_table, norm_rows, bias_columns.reshape(2, width), feed_rows]
    parts += [g_b_up.reshape(-1, width), jnp.full((1, width), penalty)]
    used = sum(part.shape[0] for part in parts)
    devices = sizes["slot"] * sizes["blk"]
    parts.append(jnp.zeros((-used % devices, width), F32))
    g_weights, packed = sum_all(
        g_weights.reshape(devices, -1, width),
        jnp.concatenate(parts, 0).reshape(devices, -1, width),
        plan,
    )
    g_weights = g_weights.reshape(3 * width, width)
    packed = packed.reshape(-1, width)[:used]
    at = types
    (
        g_ln1_gain,
        g_ln1_shift,
        g_b_query,
        g_b_value,
        g_b_out,
        g_ln2_gain,
        g_ln2_shift,
        g_b_down,
    ) = (packed[at + i] for i in range(8))
    hidden = w_up.shape[1]
    g_w_up = jnp.concatenate(
        [g_feed[at : at + width] for at in range(hidden + width, 2 * hidden + width, width)], 1
    )
    return (
        atom_out,
        pair_out,
        packed[-1, 0],
        base_grad.astype(BF16),
        pair_grad,
        packed[:types],
        g_ln1_gain,
        g_ln1_shift,
        g_weights[:width],
        g_b_query,
        g_weights[width : 2 * width],
        g_weights[2 * width :],
        g_b_value,
        g_feed[hidden : hidden + width].astype(F32),
        g_b_out,
        g_ln2_gain,
        g_ln2_shift,
        g_w_up.astype(F32),
        packed[at + 8 : used - 1].reshape(-1),
        g_feed[:hidden].astype(F32),
        g_b_down,
    )


def solution(mesh):
    atoms = P("slot", "blk", None)
    pairs = P("slot", None, "blk", None)
    sizes = {axis: mesh.shape[axis] for axis in ("slot", "blk")}
    return jax.shard_map(
        functools.partial(local, sizes),
        mesh=mesh,
        in_specs=(atoms, pairs, P("slot", "blk"), P("slot", None))
        + (P(),) * 16
        + (atoms, pairs),
        out_specs=(atoms, pairs, P(), atoms, pairs) + (P(),) * 16,
        check_vma=False,
    )
```

```python
import functools

import jax
import jax.numpy as jnp
from jax import lax
from jax.experimental import pallas as pl
from jax.experimental.pallas import tpu as pltpu
from jax.sharding import PartitionSpec as P

EPSILON = 1e-05
F32 = jnp.float32
BF16 = jnp.bfloat16
BIG = 1073741824.0
TN = (((0,), (0,)), ((), ()))
NT = (((1,), (1,)), ((), ()))
NN = (((1,), (0,)), ((), ()))
TT = (((0,), (1,)), ((), ()))
STEP = 8
CHUNK = 512
PAIR_LIMIT = 6.0
SAFE_LOGIT = 40.0


def dot(left, right, dims):
    return lax.dot_general(left, right, dims, preferred_element_type=F32)


def rounded(values):
    return lax.reduce_precision(values, 8, 7)


def unit_of(values):
    center = values - jnp.mean(values, axis=-1, keepdims=True)
    inverse = lax.rsqrt(jnp.mean(center * center, axis=-1, keepdims=True) + EPSILON)
    return center * inverse, inverse


def norm_back(upstream, unit, inverse, gain):
    scaled = upstream * gain
    first = jnp.mean(scaled, axis=-1, keepdims=True)
    second = jnp.mean(scaled * unit, axis=-1, keepdims=True)
    return inverse * (scaled - first - unit * second)


def column_sum(values):
    return jnp.sum(values, axis=0, keepdims=True)


def onehot_of(ids, types, copies):
    line = lax.broadcasted_iota(jnp.int32, (types * copies, ids.shape[1]), 0)
    hit = line == ids
    for i in range(1, copies):
        hit = hit | (line == ids + i * types)
    return jnp.where(hit, 1.0, 0.0).astype(BF16)


def upright(values):
    return jnp.broadcast_to(values.astype(F32), (8, values.shape[1])).T[:, :1]


def whole(shape):
    return pl.BlockSpec(shape, lambda *grid: (0,) * len(shape))


def by_slot(*shape):
    return pl.BlockSpec((1,) + shape, lambda s: (s,) + (0,) * len(shape))


def prepare_body(first, at, start, *refs):
    feats, types, table, gain, shift, w_key, w_value, b_value = refs[:8]
    if first:
        w_query, b_query = refs[8:10]
        base_out, normed_out, key_out, value_out, reach, far_out, query_out = refs[10:]
    else:
        far_query = refs[8]
        base_out, normed_out, key_out, value_out, reach = refs[13:]
    heads, _, cols = key_out.shape[1:]
    width = feats.shape[2]
    size = width // heads
    base = feats[0].astype(F32) + dot(
        onehot_of(types[0], table.shape[0] // 3, 3), table[...], TN
    )
    base_out[0] = base
    unit, _ = unit_of(base)
    normed = (unit * gain[...] + shift[...]).astype(BF16)
    normed_out[0] = normed

    def split_heads(values):
        return values.reshape(heads, size, values.shape[1])

    def far(values):
        return jnp.max(jnp.sum(values * values, axis=1), axis=1, keepdims=True)

    key = split_heads(dot(w_key[...], normed, TT).astype(BF16).astype(F32))
    key_out[0] = jnp.concatenate([key, key], 1).astype(BF16)
    value = split_heads(dot(w_value[...], normed, TT) + upright(b_value[...]))
    line = lax.broadcasted_iota(jnp.int32, (heads, size, cols), 1)
    value_out[0] = jnp.concatenate([value, jnp.where(line < 3, 1.0, 0.0)], 1).astype(BF16)
    if first:
        rows = query_out.shape[3]
        own = normed_out[0, pl.ds(pl.multiple_of(start[0], rows), rows), :]
        query = split_heads((dot(w_query[...], own, TT) + upright(b_query[...])).astype(BF16).astype(F32))
        scaled = query * size ** (-0.5)
        upper = scaled.astype(BF16).astype(F32)
        query_out[0] = jnp.concatenate([upper, scaled - upper], 1).astype(BF16)
        furthest = jnp.broadcast_to(far(query), far_out.shape[1:])
        far_out[0] = furthest
    else:
        furthest = far_query[0]
    reach[0] = jnp.broadcast_to(jnp.max(furthest * far(key)), reach.shape[1:])


def prepare(at, start, feats, types, shared, heads, rows, cols, extra):
    slots, part, width = feats.shape
    first = len(extra) == 2
    square = whole((width, width))
    row = whole((1, width))

    def across(s, at, start):
        return (s, at[0], 0)

    def along(s, at, start):
        return (s, 0, 0, at[0])

    def fixed(*shape):
        return pl.BlockSpec((1,) + shape, lambda s, at, start: (s,) + (0,) * len(shape))

    kept = pl.BlockSpec(memory_space=pl.ANY)
    outs = [
        ((cols, width), F32, pl.BlockSpec((1, part, width), across)),
        ((cols, width), BF16, pl.BlockSpec((1, part, width), across)),
        ((heads, 16, cols), BF16, pl.BlockSpec((1, heads, 16, part), along)),
        ((heads, 16, cols), BF16, pl.BlockSpec((1, heads, 16, part), along)),
        ((8, 128), F32, fixed(8, 128)),
    ]
    if first:
        outs.append(((heads, 128), F32, fixed(heads, 128)))
        outs.append(((heads, 16, rows), BF16, fixed(heads, 16, rows)))
    return pl.pallas_call(
        functools.partial(prepare_body, first),
        grid_spec=pltpu.PrefetchScalarGridSpec(
            num_scalar_prefetch=2,
            grid=(slots,),
            in_specs=[
                fixed(part, width),
                fixed(1, part),
                whole(shared[0].shape),
                row,
                row,
                square,
                square,
                row,
            ]
            + ([square, row] if first else [fixed(heads, 128)] + [kept] * 4),
            out_specs=[spec for _, _, spec in outs],
        ),
        out_shape=[jax.ShapeDtypeStruct((slots,) + shape, kind) for shape, kind, _ in outs],
        input_output_aliases={} if first else {11 + i: i for i in range(4)},
        compiler_params=pltpu.CompilerParams(vmem_limit_bytes=56 << 20),
        name="prepare",
    )(at, start, feats, types, *shared, *extra)


def feed_body(
    at,
    top,
    weighed,
    base,
    cotan,
    w_out,
    b_out,
    gain,
    shift,
    w_up,
    b_up,
    w_down,
    b_down,
    atom_out,
    grad_rows,
    log_total,
    resid_grad_out,
    g_weights,
    g_b_up,
    g_rows,
    total,
):
    slot = pl.program_id(0)
    heads, _, rows = weighed.shape[1:]
    width = base.shape[2]
    size = width // heads
    hidden_width = w_up.shape[1]

    @pl.when(slot == 0)
    def _():
        for ref in (total, g_b_up, g_rows):
            ref[...] = jnp.zeros_like(ref)

    totals = weighed[0, :, size : size + 1, :]
    mixed = weighed[0, :, :size, :] / totals
    logs = jnp.log(totals).reshape(heads, rows)
    for g in range(heads // STEP):
        log_total[0, g] = top[0, g] + logs[g * STEP : (g + 1) * STEP].T
    mixed_low = mixed.reshape(width, rows).astype(BF16)
    resid = base[0] + dot(mixed_low, w_out[...], TN) + b_out[...]
    unit, inverse = unit_of(resid)
    normed = (unit * gain[...] + shift[...]).astype(BF16)
    grad = cotan[0]
    down = jnp.zeros((rows, width), F32)
    back = jnp.zeros((rows, width), F32)
    for at in range(0, hidden_width, CHUNK):
        part = slice(at, at + CHUNK)
        pre = dot(normed, w_up[:, part], NN) + b_up[:, part]
        cumulative = 0.5 * (1.0 + lax.erf(pre * 0.7071067811865476))
        density = jnp.exp(-0.5 * pre * pre) * 0.3989422804014327
        hidden = (pre * cumulative).astype(BF16)
        down += dot(hidden, w_down[part, :], NN)
        total[part, :] += dot(hidden, grad, TN)
        hidden_grad = (
            dot(grad, w_down[part, :], NT) * (cumulative + pre * density)
        ).astype(BF16)
        back += dot(hidden_grad, w_up[:, part], NT)
        total[hidden_width + width + at : hidden_width + 2 * width + at] += dot(
            normed, hidden_grad, TN
        )
        g_b_up[:, part] += column_sum(hidden_grad.astype(F32))
    atom_out[0] = (resid + down + b_down[...]).astype(BF16)
    resid_grad = grad.astype(F32) + norm_back(back, unit, inverse, gain[...])
    resid_grad_out[0] = resid_grad
    low = resid_grad.astype(BF16)
    total[hidden_width : hidden_width + width] += dot(mixed_low, low, NN)
    g_rows[0:1] += column_sum(low.astype(F32))
    g_rows[1:2] += column_sum(back * unit)
    g_rows[2:3] += column_sum(back)
    g_rows[3:4] += column_sum(grad.astype(F32))
    mixed_grad = dot(w_out[...], low, NT).astype(BF16).astype(F32).reshape(heads, size, rows)
    delta = -jnp.sum(mixed_grad * mixed, axis=1, keepdims=True)
    first = delta.astype(BF16).astype(F32)
    second = (delta - first).astype(BF16).astype(F32)
    line = lax.broadcasted_iota(jnp.int32, (heads, size, rows), 1)
    extra = jnp.where(
        line == 0,
        first,
        jnp.where(line == 1, second, jnp.where(line == 2, delta - first - second, 0.0)),
    )
    grad_rows[0] = jnp.concatenate([mixed_grad, extra], 1).astype(BF16)

    @pl.when(slot == pl.num_programs(0) - 1)
    def _():
        g_weights[...] = total[...].astype(BF16)


def feed(at, top, weighed, base, cotan, w_out, b_out, gain, shift, w_up, b_up, w_down, b_down):
    slots, heads, _, rows = weighed.shape
    width, hidden = w_up.shape
    row = whole((1, width))
    own = [
        ((rows, width), BF16),
        ((heads, 16, rows), BF16),
        ((heads // STEP, rows, STEP), F32),
        ((rows, width), F32),
    ]
    shared = [
        ((2 * hidden + width, width), BF16),
        ((1, hidden), F32),
        ((4, width), F32),
    ]

    def by_slot(*shape):
        return pl.BlockSpec((1,) + shape, lambda s, at: (s,) + (0,) * len(shape))

    return pl.pallas_call(
        feed_body,
        grid_spec=pltpu.PrefetchScalarGridSpec(
            num_scalar_prefetch=1,
            grid=(slots,),
            in_specs=[
                by_slot(heads // STEP, rows, STEP),
                by_slot(heads, 16, rows),
                pl.BlockSpec((1, rows, width), lambda s, at: (s, at[0], 0)),
            by_slot(rows, width),
            whole((width, width)),
            row,
            row,
            row,
            whole((width, hidden)),
            whole((1, hidden)),
            whole((hidden, width)),
            row,
        ],
        out_specs=[by_slot(*shape) for shape, _ in own] + [whole(shape) for shape, _ in shared],
            scratch_shapes=[pltpu.VMEM(shared[0][0], F32)],
        ),
        out_shape=[jax.ShapeDtypeStruct((slots,) + shape, kind) for shape, kind in own]
        + [jax.ShapeDtypeStruct(shape, kind) for shape, kind in shared],
        compiler_params=pltpu.CompilerParams(vmem_limit_bytes=60 << 20),
        name="feed",
    )(at, top, weighed, base, cotan, w_out, b_out, gain, shift, w_up, b_up, w_down, b_down)


def finish_body(
    start,
    query_part,
    key_part,
    value_part,
    base,
    normed,
    types,
    resid_grad,
    gain,
    w_query,
    w_key,
    w_value,
    feed_rows,
    g_b_up,
    pen_tile,
    *rest,
):
    *backs, g_weights, short, g_table, g_rows, g_columns, g_turned, upstream = rest
    slot = pl.program_id(0)
    rows, width = resid_grad.shape[1:]
    cols = base.shape[1]
    heads, size = query_part.shape[1:3]
    own = pl.ds(pl.multiple_of(start[0], rows), rows)

    @pl.when(slot == 0)
    def _():
        for ref in (g_turned, g_table, g_rows, g_columns):
            ref[...] = jnp.zeros_like(ref)

    query_wide = (query_part[0] * size ** (-0.5)).reshape(width, rows)
    value_wide = value_part[0].reshape(width, cols)
    query_grad = query_wide.astype(BF16)
    key_grad = key_part[0].reshape(width, cols).astype(BF16)
    value_grad = value_wide.astype(BF16)
    g_turned[0] += dot(query_grad, normed[0, own, :], NN)
    g_turned[1] += dot(key_grad, normed[0], NN)
    g_turned[2] += dot(value_grad, normed[0], NN)
    g_columns[0] += jnp.sum(query_grad.astype(F32), axis=1, keepdims=True)
    g_columns[1] += jnp.sum(value_wide, axis=1, keepdims=True)
    upstream[...] = dot(key_grad, w_key[...], TT) + dot(value_grad, w_value[...], TT)
    upstream[own, :] += dot(query_grad, w_query[...], TT)
    unit, inverse = unit_of(base[0])
    received = upstream[...]
    g_rows[0:1] += column_sum(received * unit)
    g_rows[1:2] += column_sum(received)
    upstream[...] = norm_back(received, unit, inverse, gain[...])
    if len(backs) == 1:
        backs[0][0] = upstream[...]
    else:
        backs[1][0] = upstream[pl.ds(pl.multiple_of(start[1], rows), rows), :].astype(BF16)
    upstream[own, :] += resid_grad[0]
    if len(backs) == 2:
        backs[0][0] = upstream[own, :]
    total = upstream[...]
    upper = total.astype(BF16)
    lower = (total - upper.astype(F32)).astype(BF16)
    onehot = onehot_of(types[0], g_table.shape[0], 1)
    g_table[...] += dot(onehot, upper, NN) + dot(onehot, lower, NN)

    @pl.when(slot == pl.num_programs(0) - 1)
    def _():
        for i in range(3):
            g_weights[i * width : (i + 1) * width] = g_turned[i].T
        lines = [g_table[...], g_rows[...]]
        lines += [jnp.broadcast_to(g_columns[i], (width, 128)).T[:1] for i in range(2)]
        lines += [feed_rows[...]]
        lines += [g_b_up[:, i : i + width] for i in range(0, g_b_up.shape[1], width)]
        lines += [jnp.full((1, width), 0.5 * jnp.sum(pen_tile[...]))]
        at = 0
        short[...] = jnp.zeros_like(short)
        for values in lines:
            short[at : at + values.shape[0]] = values
            at += values.shape[0]


def finish(
    start,
    query_part,
    key_part,
    value_part,
    base,
    normed,
    types,
    resid_grad,
    gain,
    w_query,
    w_key,
    w_value,
    feed_rows,
    g_b_up,
    pen_tile,
    type_count,
    lines,
    halves,
):
    slots, heads, size, rows = query_part.shape
    cols, width = base.shape[1:]
    square = whole((width, width))
    backs = [((rows, width), F32), ((rows, width), BF16)] if halves else [((cols, width), F32)]
    shared = [((3 * width, width), F32), ((lines, width), F32)]
    return pl.pallas_call(
        finish_body,
        grid=(slots,),
        in_specs=[
            pl.BlockSpec(memory_space=pltpu.SMEM),
            by_slot(heads, size, rows),
            by_slot(heads, size, cols),
            by_slot(heads, size, cols),
            by_slot(cols, width),
            by_slot(cols, width),
            by_slot(1, cols),
            by_slot(rows, width),
            whole((1, width)),
            square,
            square,
            square,
            whole(feed_rows.shape),
            whole(g_b_up.shape),
            whole(pen_tile.shape),
        ],
        out_specs=[by_slot(*shape) for shape, _ in backs] + [whole(shape) for shape, _ in shared],
        out_shape=[jax.ShapeDtypeStruct((slots,) + shape, kind) for shape, kind in backs]
        + [jax.ShapeDtypeStruct(shape, kind) for shape, kind in shared],
        scratch_shapes=[
            pltpu.VMEM((type_count, width), F32),
            pltpu.VMEM((2, width), F32),
            pltpu.VMEM((2, width, 1), F32),
            pltpu.VMEM((3, width, width), F32),
            pltpu.VMEM((cols, width), F32),
        ],
        compiler_params=pltpu.CompilerParams(vmem_limit_bytes=56 << 20),
        name="finish",
    )(
        start,
        query_part,
        key_part,
        value_part,
        base,
        normed,
        types,
        resid_grad,
        gain,
        w_query,
        w_key,
        w_value,
        feed_rows,
        g_b_up,
        pen_tile,
    )


def forward_body(
    safe, pf, query, key, value, row_ids, col_ids, mixed, top, mask, bias, kept
):
    slot = pl.program_id(0)
    group = pl.program_id(1)
    heads = pf.shape[1]

    @pl.when(group == 0)
    def _():
        same = upright(row_ids[0]) == col_ids[0].astype(F32)
        mask[...] = jnp.where(same, 1.0, 0.0).astype(BF16)
        bias[...] = jnp.where(same, 0.0, -BIG)

    def logits_of(h):
        return dot(query[0, h], key[0, h], TN) + pf[0, h].astype(F32)

    def weigh(h, spot):
        mixed[0, h] = dot(value[0, h], kept[spot], NT)

    is_safe = safe[slot] == 1

    @pl.when(is_safe)
    def _():
        top[...] = jnp.zeros_like(top)

        for h in range(heads):
            kept[h % 2] = jnp.exp(logits_of(h)).astype(BF16) * mask[...]
            if h:
                weigh(h - 1, (h - 1) % 2)
        weigh(heads - 1, (heads - 1) % 2)

    @pl.when(jnp.logical_not(is_safe))
    def _():
        def block(i, carry):
            for u in range(STEP):
                h = i * STEP + u
                masked = logits_of(h) + bias[...]
                highest = jnp.max(masked, axis=1, keepdims=True)
                top[0, i, :, u : u + 1] = highest
                kept[0] = jnp.exp(masked - highest).astype(BF16)
                weigh(h, 0)
            return carry

        lax.fori_loop(0, heads // STEP, block, 0)


def attend(safe, pf, query, key, value, row_ids, col_ids, per_step):
    slots, heads, rows, cols = pf.shape

    def by_head(height, width):
        return pl.BlockSpec((1, per_step, height, width), lambda s, g: (s, g, 0, 0))

    return pl.pallas_call(
        forward_body,
        grid=(slots, heads // per_step),
        in_specs=[
            pl.BlockSpec(memory_space=pltpu.SMEM),
            by_head(rows, cols),
            by_head(16, rows),
            by_head(16, cols),
            by_head(16, cols),
            pl.BlockSpec((1, 1, rows), lambda s, g: (s, 0, 0)),
            pl.BlockSpec((1, 1, cols), lambda s, g: (s, 0, 0)),
        ],
        out_specs=[
            by_head(16, rows),
            pl.BlockSpec((1, per_step // STEP, rows, STEP), lambda s, g: (s, g, 0, 0)),
        ],
        out_shape=[
            jax.ShapeDtypeStruct((slots, heads, 16, rows), F32),
            jax.ShapeDtypeStruct((slots, heads // STEP, rows, STEP), F32),
        ],
        scratch_shapes=[
            pltpu.VMEM((rows, cols), BF16),
            pltpu.VMEM((rows, cols), F32),
            pltpu.VMEM((2, rows, cols), BF16),
        ],
        compiler_params=pltpu.CompilerParams(vmem_limit_bytes=56 << 20),
        name="attend",
    )(safe, pf, query, key, value, row_ids, col_ids)


def backward_body(
    safe,
    scale,
    pf,
    cotan,
    query,
    key,
    grad,
    value,
    log_total,
    row_ids,
    col_ids,
    pair_out,
    pair_grad,
    query_grad,
    key_grad,
    value_grad,
    penalty,
    weight,
    mask,
    bias,
    probs,
):
    slot = pl.program_id(0)
    group = pl.program_id(1)
    heads = pf.shape[1]
    rows, cols = pf.shape[2:]

    @pl.when(group == 0)
    def _():
        same = upright(row_ids[0]) == col_ids[0].astype(F32)
        weight[...] = jnp.where(same, scale[0], 0.0).astype(BF16)
        mask[...] = jnp.where(same, 1.0, 0.0).astype(BF16)
        bias[...] = jnp.where(same, 0.0, -BIG)

    @pl.when((group == 0) & (slot == 0))
    def _():
        penalty[...] = jnp.zeros_like(penalty)

    def pairs(i, u, safe):
        h = i * STEP + u
        logits = dot(query[0, h], key[0, h], TN) + pf[0, h].astype(F32)
        logits_low = logits.astype(BF16)
        pair_out[0, h] = logits_low
        probs_grad = dot(grad[0, h], value[0, h], TN).astype(BF16)
        shifted = logits - log_total[0, i, :, u : u + 1]
        if safe:
            prob = jnp.exp(shifted).astype(BF16) * mask[...]
        else:
            prob = jnp.exp(shifted + bias[...]).astype(BF16)
        probs[h % 2] = prob
        pen_grad = logits_low * weight[...]
        pair_grad[0, h] = prob * probs_grad + (cotan[0, h] + pen_grad)
        squares = pen_grad * logits_low
        while squares.shape[0] > 16:
            half = squares.shape[0] // 2
            squares = squares[:half] + squares[half:]
        penalty[...] += squares.astype(F32)

    def sums(h, spot):
        upper = dot(query[0, h], pair_grad[0, h], NN)
        key_grad[0, h] = upper[:8] + upper[8:]
        value_grad[0, h] = dot(grad[0, h], probs[spot], NN)[:8]
        query_grad[0, h] = dot(key[0, h], pair_grad[0, h], NT)[:8]

    is_safe = safe[slot] == 1

    @pl.when(is_safe)
    def _():
        for h in range(heads):
            pairs(h // STEP, h % STEP, True)
            if h:
                sums(h - 1, (h - 1) % 2)
        sums(heads - 1, (heads - 1) % 2)

    @pl.when(jnp.logical_not(is_safe))
    def _():
        for h in range(heads):
            pairs(h // STEP, h % STEP, False)
            sums(h, h % 2)


def attend_back(
    safe, scale, pf, cotan, query, key, grad, value, log_total, row_ids, col_ids, per_step
):
    slots, heads, rows, cols = pf.shape

    def by_head(height, width):
        return pl.BlockSpec((1, per_step, height, width), lambda s, g: (s, g, 0, 0))

    return pl.pallas_call(
        backward_body,
        grid=(slots, heads // per_step),
        in_specs=[
            pl.BlockSpec(memory_space=pltpu.SMEM),
            pl.BlockSpec(memory_space=pltpu.SMEM),
            by_head(rows, cols),
            by_head(rows, cols),
            by_head(16, rows),
            by_head(16, cols),
            by_head(16, rows),
            by_head(16, cols),
            pl.BlockSpec((1, per_step // STEP, rows, STEP), lambda s, g: (s, g, 0, 0)),
            pl.BlockSpec((1, 1, rows), lambda s, g: (s, 0, 0)),
            pl.BlockSpec((1, 1, cols), lambda s, g: (s, 0, 0)),
        ],
        out_specs=[
            by_head(rows, cols),
            by_head(rows, cols),
            by_head(8, rows),
            by_head(8, cols),
            by_head(8, cols),
            pl.BlockSpec((16, cols), lambda s, g: (0, 0)),
        ],
        out_shape=[
            jax.ShapeDtypeStruct((slots, heads, rows, cols), BF16),
            jax.ShapeDtypeStruct((slots, heads, rows, cols), BF16),
            jax.ShapeDtypeStruct((slots, heads, 8, rows), F32),
            jax.ShapeDtypeStruct((slots, heads, 8, cols), F32),
            jax.ShapeDtypeStruct((slots, heads, 8, cols), F32),
            jax.ShapeDtypeStruct((16, cols), F32),
        ],
        scratch_shapes=[
            pltpu.VMEM((rows, cols), BF16),
            pltpu.VMEM((rows, cols), BF16),
            pltpu.VMEM((rows, cols), F32),
            pltpu.VMEM((2, rows, cols), BF16),
        ],
        compiler_params=pltpu.CompilerParams(vmem_limit_bytes=60 << 20),
        name="attend_back",
    )(safe, scale, pf, cotan, query, key, grad, value, log_total, row_ids, col_ids)


def flips(sizes):
    found = []
    for axis in ("slot", "blk"):
        bit = 1
        while bit < sizes[axis]:
            found.append((axis, bit))
            bit *= 2
    return found


def swap(values, sizes, axis, bit):
    return lax.ppermute(values, axis, [(i, i ^ bit) for i in range(sizes[axis])])


def butterfly(values, sizes, axes=("slot", "blk")):
    for axis, bit in flips(sizes):
        if axis in axes:
            values = values + swap(values, sizes, axis, bit)
    return values


def step_plan(sizes):
    whole = sizes["slot"] * sizes["blk"]
    blk = sizes["blk"]
    slot_at = lax.axis_index("slot")
    blk_at = lax.axis_index("blk")

    def partner(device, axis, bit):
        s, b = divmod(device, blk)
        return (s ^ bit) * blk + b if axis == "slot" else s * blk + (b ^ bit)

    def bit_of(axis, bit):
        return ((slot_at if axis == "slot" else blk_at) // bit) % 2

    def plain(axis, bit):
        return ([(d, partner(d, axis, bit)) for d in range(whole)], bit_of(axis, bit))

    def mixed(even, odd):
        pairs = [(d, partner(d, *(even if (d // blk) % 2 == 0 else odd))) for d in range(whole)]
        return (pairs, jnp.where(slot_at % 2 == 0, bit_of(*even), bit_of(*odd)))

    steps = flips(sizes)
    core, rest = steps[0], steps[1:]
    near_y, near_x = ("slot", 2), ("blk", 1)
    plan = [plain(*core)]
    if near_y in rest and near_x in rest:
        rest = [step for step in rest if step not in (near_y, near_x)]
        plan += [mixed(near_x, near_y), mixed(near_y, near_x)]
    return plan + [plain(*step) for step in rest]


def sum_all(wide, small, plan):
    joint = ("slot", "blk")
    rows, extra = wide.shape[1], small.shape[1]

    def parcel(wide, small):
        upper = rounded(small)
        parts = [wide.astype(BF16), upper.astype(BF16), (small - upper).astype(BF16)]
        return jnp.concatenate(parts, 1)

    def unpack(values):
        values = values.astype(F32)
        return values[:, :rows], values[:, rows : rows + extra] + values[:, rows + extra :]

    def pick(values, half):
        halves = values.reshape((2, values.shape[0] // 2) + values.shape[1:])
        return lax.dynamic_index_in_dim(halves, half, 0, keepdims=False)

    for pairs, half in plan:
        away = parcel(pick(wide, 1 - half), pick(small, 1 - half))
        came_wide, came_small = unpack(lax.ppermute(away, joint, pairs))
        wide = pick(wide, half) + came_wide
        small = pick(small, half) + came_small
    values = parcel(wide, small)
    for pairs, half in plan[::-1]:
        came = lax.ppermute(values, joint, pairs)
        values = jnp.where(
            half == 0,
            jnp.concatenate([values, came], 0),
            jnp.concatenate([came, values], 0),
        )
    return unpack(values)


def sum_wide(values, sizes, after):
    joint = ("slot", "blk")
    count = sizes["slot"] * sizes["blk"]
    terms = lax.all_to_all(values, joint, 0, 0, tiled=True)
    terms, after = lax.optimization_barrier((terms, after))
    terms = terms.reshape((count, values.shape[0] // count, values.shape[1]))
    total = jnp.sum(terms.astype(F32), axis=0).astype(BF16)
    return lax.all_gather(total, joint, tiled=True), after


def local(
    sizes,
    atom_feats,
    pair_feats,
    type_ids,
    mol_lengths,
    type_table,
    ln1_gain,
    ln1_shift,
    w_query,
    b_query,
    w_key,
    w_value,
    b_value,
    w_out,
    b_out,
    ln2_gain,
    ln2_shift,
    w_up,
    b_up,
    w_down,
    b_down,
    atom_cotan,
    pair_cotan,
):
    slots, rows, width = atom_feats.shape
    heads = pair_feats.shape[1]
    cols = pair_feats.shape[3]
    types = type_table.shape[0]
    blk_at = lax.axis_index("blk")
    row_start = blk_at * rows
    plan = step_plan(sizes)

    def own(values, axis=1):
        return lax.dynamic_slice_in_dim(values, row_start, rows, axis)

    bounds = jnp.cumsum(mol_lengths, axis=1)
    places = jnp.arange(cols, dtype=jnp.int32)
    mol_ids = jnp.sum((places[None, :, None] >= bounds[:, None, :]).astype(jnp.int32), axis=2)
    row_mols = own(mol_ids)
    row_ids = row_mols[:, None, :]
    col_ids = mol_ids[:, None, :]

    first = rounded(type_table)
    second = rounded(type_table - first)
    table = jnp.concatenate([first, second, type_table - first - second], 0).astype(BF16)
    start = row_start.astype(jnp.int32).reshape(1)
    here = blk_at.astype(jnp.int32).reshape(1)

    def line(values):
        return values.reshape(1, -1)

    shared = (table, line(ln1_gain), line(ln1_shift), w_key, w_value, line(b_value))
    asking = (w_query, line(b_query))

    def safe_of(reach):
        furthest = (width // heads) ** (-0.5) * jnp.sqrt(reach[:, 0, 0]) + PAIR_LIMIT
        return (furthest <= SAFE_LOGIT).astype(jnp.int32)

    count = jnp.sum(mol_lengths * mol_lengths).astype(F32).reshape(1, 1)
    if sizes["blk"] == 2:
        there = 1 - here
        came_feats = swap(atom_feats, sizes, "blk", 1)
        came_types = swap(type_ids, sizes, "blk", 1)
        near = [swap(count, sizes, "slot", bit) for bit in (1, 2, 3)]
        base, normed, key_rows, value_rows, reach, far_query, query_rows = prepare(
            here,
            jnp.zeros((1,), jnp.int32),
            atom_feats,
            type_ids[:, None, :],
            shared,
            heads,
            rows,
            cols,
            asking,
        )
        safe = safe_of(reach)
        near, reach = lax.optimization_barrier((near, reach))
        count = count + near[0] + (near[1] + near[2])
        far = [swap(count, sizes, "slot", bit) for bit in range(4, sizes["slot"], 4)]
        base, normed, key_rows, value_rows, reach = prepare(
            there,
            start,
            came_feats,
            came_types[:, None, :],
            shared,
            heads,
            rows,
            cols,
            (far_query, base, normed, key_rows, value_rows),
        )
        safe = safe * safe_of(reach)
        far, safe = lax.optimization_barrier((far, safe))
        pair_total = count + sum(far)
        all_types = jnp.where(
            blk_at == 0,
            jnp.concatenate([type_ids, came_types], 1),
            jnp.concatenate([came_types, type_ids], 1),
        )
    else:
        feats = lax.all_gather(atom_feats, "blk", axis=1, tiled=True)
        all_types = lax.all_gather(type_ids, "blk", axis=1, tiled=True)
        zero = jnp.zeros((1,), jnp.int32)
        base, normed, key_rows, value_rows, reach, _, query_rows = prepare(
            zero,
            start,
            feats,
            all_types[:, None, :],
            shared,
            heads,
            rows,
            cols,
            asking,
        )
        safe = safe_of(reach)
        pair_total = butterfly(count, sizes, ("slot",))
    pen_scale = (2.0 / pair_total).reshape(1)
    weighed, top = attend(
        safe, pair_feats, query_rows, key_rows, value_rows, row_ids, col_ids, 16
    )
    types_row = all_types[:, None, :]

    atom_out, grad_rows, log_total, resid_grad, g_feed, g_b_up, feed_rows = feed(
        here,
        top,
        weighed,
        base,
        atom_cotan,
        w_out,
        line(b_out),
        line(ln2_gain),
        line(ln2_shift),
        w_up,
        line(b_up),
        w_down,
        line(b_down),
    )

    pair_out, pair_grad, query_part, key_part, value_part, pen_tile = attend_back(
        safe,
        pen_scale,
        pair_feats,
        pair_cotan,
        query_rows,
        key_rows,
        grad_rows,
        value_rows,
        log_total,
        row_ids,
        col_ids,
        16,
    )

    devices = sizes["slot"] * sizes["blk"]
    used = types + 9 + g_b_up.shape[1] // width
    halves = sizes["blk"] == 2
    *backs, g_weights, short = finish(
        jnp.concatenate([start, rows - start]),
        query_part,
        key_part,
        value_part,
        base,
        normed,
        types_row,
        resid_grad,
        line(ln1_gain),
        w_query,
        w_key,
        w_value,
        feed_rows,
        g_b_up,
        pen_tile,
        types,
        used + -used % devices,
        halves,
    )
    g_feed, short = sum_wide(g_feed, sizes, short)
    if halves:
        base_grad = backs[0] + swap(backs[1], sizes, "blk", 1).astype(F32)
    else:
        base_grad = resid_grad + lax.psum_scatter(backs[0], "blk", scatter_dimension=1, tiled=True)
    hidden = w_up.shape[1]
    g_w_up = jnp.concatenate(
        [g_feed[at : at + width] for at in range(hidden + width, 2 * hidden + width, width)], 1
    ).astype(F32)
    g_w_down = g_feed[:hidden].astype(F32)
    g_w_out = g_feed[hidden : hidden + width].astype(F32)
    g_weights, packed = sum_all(
        g_weights.reshape(devices, -1, width), short.reshape(devices, -1, width), plan
    )
    g_weights = g_weights.reshape(3 * width, width)
    packed = packed.reshape(-1, width)[:used]
    at = types
    (
        g_ln1_gain,
        g_ln1_shift,
        g_b_query,
        g_b_value,
        g_b_out,
        g_ln2_gain,
        g_ln2_shift,
        g_b_down,
    ) = (packed[at + i] for i in range(8))
    return (
        atom_out,
        pair_out,
        packed[-1, 0],
        base_grad.astype(BF16),
        pair_grad,
        packed[:types],
        g_ln1_gain,
        g_ln1_shift,
        g_weights[:width],
        g_b_query,
        g_weights[width : 2 * width],
        g_weights[2 * width :],
        g_b_value,
        g_w_out,
        g_b_out,
        g_ln2_gain,
        g_ln2_shift,
        g_w_up,
        packed[at + 8 : used - 1].reshape(-1),
        g_w_down,
        g_b_down,
    )


def solution(mesh):
    atoms = P("slot", "blk", None)
    pairs = P("slot", None, "blk", None)
    sizes = {axis: mesh.shape[axis] for axis in ("slot", "blk")}
    return jax.shard_map(
        functools.partial(local, sizes),
        mesh=mesh,
        in_specs=(atoms, pairs, P("slot", "blk"), P("slot", None))
        + (P(),) * 16
        + (atoms, pairs),
        out_specs=(atoms, pairs, P(), atoms, pairs) + (P(),) * 16,
        check_vma=False,
    )
```

```python
import functools

import jax
import jax.numpy as jnp
from jax import lax
from jax.experimental import pallas as pl
from jax.experimental.pallas import tpu as pltpu
from jax.sharding import PartitionSpec as P

EPSILON = 1e-05
F32 = jnp.float32
BF16 = jnp.bfloat16
BIG = 1073741824.0
TN = (((0,), (0,)), ((), ()))
NT = (((1,), (1,)), ((), ()))
NN = (((1,), (0,)), ((), ()))
TT = (((0,), (1,)), ((), ()))
STEP = 8
CHUNK = 512
PAIR_LIMIT = 6.0
SAFE_LOGIT = 40.0


def dot(left, right, dims):
    return lax.dot_general(left, right, dims, preferred_element_type=F32)


def rounded(values):
    return lax.reduce_precision(values, 8, 7)


def unit_of(values):
    center = values - jnp.mean(values, axis=-1, keepdims=True)
    inverse = lax.rsqrt(jnp.mean(center * center, axis=-1, keepdims=True) + EPSILON)
    return center * inverse, inverse


def norm_back(upstream, unit, inverse, gain):
    scaled = upstream * gain
    first = jnp.mean(scaled, axis=-1, keepdims=True)
    second = jnp.mean(scaled * unit, axis=-1, keepdims=True)
    return inverse * (scaled - first - unit * second)


def column_sum(values):
    return jnp.sum(values, axis=0, keepdims=True)


def onehot_of(ids, types, copies):
    line = lax.broadcasted_iota(jnp.int32, (types * copies, ids.shape[1]), 0)
    hit = line == ids
    for i in range(1, copies):
        hit = hit | (line == ids + i * types)
    return jnp.where(hit, 1.0, 0.0).astype(BF16)


def upright(values):
    return jnp.broadcast_to(values.astype(F32), (8, values.shape[1])).T[:, :1]


def whole(shape):
    return pl.BlockSpec(shape, lambda *grid: (0,) * len(shape))


def by_slot(*shape):
    return pl.BlockSpec((1,) + shape, lambda s: (s,) + (0,) * len(shape))


def prepare_body(first, at, start, *refs):
    feats, types, table, gain, shift, w_key, w_value, b_value = refs[:8]
    if first:
        w_query, b_query = refs[8:10]
        base_out, normed_out, key_out, value_out, reach, far_out, query_out = refs[10:]
    else:
        far_query = refs[8]
        base_out, normed_out, key_out, value_out, reach = refs[13:]
    heads, _, cols = key_out.shape[1:]
    width = feats.shape[2]
    size = width // heads
    base = feats[0].astype(F32) + dot(
        onehot_of(types[0], table.shape[0] // 3, 3), table[...], TN
    )
    base_out[0] = base
    unit, _ = unit_of(base)
    normed = (unit * gain[...] + shift[...]).astype(BF16)
    normed_out[0] = normed

    def split_heads(values):
        return values.reshape(heads, size, values.shape[1])

    def far(values):
        return jnp.max(jnp.sum(values * values, axis=1), axis=1, keepdims=True)

    key = split_heads(dot(w_key[...], normed, TT).astype(BF16).astype(F32))
    key_out[0] = jnp.concatenate([key, key], 1).astype(BF16)
    value = split_heads(dot(w_value[...], normed, TT) + upright(b_value[...]))
    line = lax.broadcasted_iota(jnp.int32, (heads, size, cols), 1)
    value_out[0] = jnp.concatenate([value, jnp.where(line < 3, 1.0, 0.0)], 1).astype(BF16)
    if first:
        rows = query_out.shape[3]
        own = normed_out[0, pl.ds(pl.multiple_of(start[0], rows), rows), :]
        query = split_heads((dot(w_query[...], own, TT) + upright(b_query[...])).astype(BF16).astype(F32))
        scaled = query * size ** (-0.5)
        upper = scaled.astype(BF16).astype(F32)
        query_out[0] = jnp.concatenate([upper, scaled - upper], 1).astype(BF16)
        furthest = jnp.broadcast_to(far(query), far_out.shape[1:])
        far_out[0] = furthest
    else:
        furthest = far_query[0]
    reach[0] = jnp.broadcast_to(jnp.max(furthest * far(key)), reach.shape[1:])


def prepare(at, start, feats, types, shared, heads, rows, cols, extra):
    slots, part, width = feats.shape
    first = len(extra) == 2
    square = whole((width, width))
    row = whole((1, width))

    def across(s, at, start):
        return (s, at[0], 0)

    def along(s, at, start):
        return (s, 0, 0, at[0])

    def fixed(*shape):
        return pl.BlockSpec((1,) + shape, lambda s, at, start: (s,) + (0,) * len(shape))

    kept = pl.BlockSpec(memory_space=pl.ANY)
    outs = [
        ((cols, width), F32, pl.BlockSpec((1, part, width), across)),
        ((cols, width), BF16, pl.BlockSpec((1, part, width), across)),
        ((heads, 16, cols), BF16, pl.BlockSpec((1, heads, 16, part), along)),
        ((heads, 16, cols), BF16, pl.BlockSpec((1, heads, 16, part), along)),
        ((8, 128), F32, fixed(8, 128)),
    ]
    if first:
        outs.append(((heads, 128), F32, fixed(heads, 128)))
        outs.append(((heads, 16, rows), BF16, fixed(heads, 16, rows)))
    return pl.pallas_call(
        functools.partial(prepare_body, first),
        grid_spec=pltpu.PrefetchScalarGridSpec(
            num_scalar_prefetch=2,
            grid=(slots,),
            in_specs=[
                fixed(part, width),
                fixed(1, part),
                whole(shared[0].shape),
                row,
                row,
                square,
                square,
                row,
            ]
            + ([square, row] if first else [fixed(heads, 128)] + [kept] * 4),
            out_specs=[spec for _, _, spec in outs],
        ),
        out_shape=[jax.ShapeDtypeStruct((slots,) + shape, kind) for shape, kind, _ in outs],
        input_output_aliases={} if first else {11 + i: i for i in range(4)},
        compiler_params=pltpu.CompilerParams(vmem_limit_bytes=56 << 20),
        name="prepare",
    )(at, start, feats, types, *shared, *extra)


def feed_body(
    at,
    top,
    weighed,
    base,
    cotan,
    w_out,
    b_out,
    gain,
    shift,
    w_up,
    b_up,
    w_down,
    b_down,
    atom_out,
    grad_rows,
    log_total,
    resid_grad_out,
    g_weights,
    g_b_up,
    g_rows,
    total,
):
    slot = pl.program_id(0)
    heads, _, rows = weighed.shape[1:]
    width = base.shape[2]
    size = width // heads
    hidden_width = w_up.shape[1]

    @pl.when(slot == 0)
    def _():
        for ref in (total, g_b_up, g_rows):
            ref[...] = jnp.zeros_like(ref)

    totals = weighed[0, :, size : size + 1, :]
    mixed = weighed[0, :, :size, :] / totals
    logs = jnp.log(totals).reshape(heads, rows)
    for g in range(heads // STEP):
        log_total[0, g] = top[0, g] + logs[g * STEP : (g + 1) * STEP].T
    mixed_low = mixed.reshape(width, rows).astype(BF16)
    resid = base[0] + dot(mixed_low, w_out[...], TN) + b_out[...]
    unit, inverse = unit_of(resid)
    normed = (unit * gain[...] + shift[...]).astype(BF16)
    grad = cotan[0]
    down = jnp.zeros((rows, width), F32)
    back = jnp.zeros((rows, width), F32)
    for at in range(0, hidden_width, CHUNK):
        part = slice(at, at + CHUNK)
        pre = dot(normed, w_up[:, part], NN) + b_up[:, part]
        cumulative = 0.5 * (1.0 + lax.erf(pre * 0.7071067811865476))
        density = jnp.exp(-0.5 * pre * pre) * 0.3989422804014327
        hidden = (pre * cumulative).astype(BF16)
        down += dot(hidden, w_down[part, :], NN)
        total[part, :] += dot(hidden, grad, TN)
        hidden_grad = (
            dot(grad, w_down[part, :], NT) * (cumulative + pre * density)
        ).astype(BF16)
        back += dot(hidden_grad, w_up[:, part], NT)
        total[hidden_width + width + at : hidden_width + 2 * width + at] += dot(
            normed, hidden_grad, TN
        )
        g_b_up[:, part] += column_sum(hidden_grad.astype(F32))
    atom_out[0] = (resid + down + b_down[...]).astype(BF16)
    resid_grad = grad.astype(F32) + norm_back(back, unit, inverse, gain[...])
    resid_grad_out[0] = resid_grad
    low = resid_grad.astype(BF16)
    total[hidden_width : hidden_width + width] += dot(mixed_low, low, NN)
    g_rows[0:1] += column_sum(low.astype(F32))
    g_rows[1:2] += column_sum(back * unit)
    g_rows[2:3] += column_sum(back)
    g_rows[3:4] += column_sum(grad.astype(F32))
    mixed_grad = dot(w_out[...], low, NT).astype(BF16).astype(F32).reshape(heads, size, rows)
    delta = -jnp.sum(mixed_grad * mixed, axis=1, keepdims=True)
    first = delta.astype(BF16).astype(F32)
    second = (delta - first).astype(BF16).astype(F32)
    line = lax.broadcasted_iota(jnp.int32, (heads, size, rows), 1)
    extra = jnp.where(
        line == 0,
        first,
        jnp.where(line == 1, second, jnp.where(line == 2, delta - first - second, 0.0)),
    )
    grad_rows[0] = jnp.concatenate([mixed_grad, extra], 1).astype(BF16)

    @pl.when(slot == pl.num_programs(0) - 1)
    def _():
        g_weights[...] = total[...].astype(BF16)


def feed(at, top, weighed, base, cotan, w_out, b_out, gain, shift, w_up, b_up, w_down, b_down):
    slots, heads, _, rows = weighed.shape
    width, hidden = w_up.shape
    row = whole((1, width))
    own = [
        ((rows, width), BF16),
        ((heads, 16, rows), BF16),
        ((heads // STEP, rows, STEP), F32),
        ((rows, width), F32),
    ]
    shared = [
        ((2 * hidden + width, width), BF16),
        ((1, hidden), F32),
        ((4, width), F32),
    ]

    def by_slot(*shape):
        return pl.BlockSpec((1,) + shape, lambda s, at: (s,) + (0,) * len(shape))

    return pl.pallas_call(
        feed_body,
        grid_spec=pltpu.PrefetchScalarGridSpec(
            num_scalar_prefetch=1,
            grid=(slots,),
            in_specs=[
                by_slot(heads // STEP, rows, STEP),
                by_slot(heads, 16, rows),
                pl.BlockSpec((1, rows, width), lambda s, at: (s, at[0], 0)),
            by_slot(rows, width),
            whole((width, width)),
            row,
            row,
            row,
            whole((width, hidden)),
            whole((1, hidden)),
            whole((hidden, width)),
            row,
        ],
        out_specs=[by_slot(*shape) for shape, _ in own] + [whole(shape) for shape, _ in shared],
            scratch_shapes=[pltpu.VMEM(shared[0][0], F32)],
        ),
        out_shape=[jax.ShapeDtypeStruct((slots,) + shape, kind) for shape, kind in own]
        + [jax.ShapeDtypeStruct(shape, kind) for shape, kind in shared],
        compiler_params=pltpu.CompilerParams(vmem_limit_bytes=60 << 20),
        name="feed",
    )(at, top, weighed, base, cotan, w_out, b_out, gain, shift, w_up, b_up, w_down, b_down)


def finish_body(
    start,
    query_part,
    key_part,
    value_part,
    base,
    normed,
    types,
    resid_grad,
    gain,
    w_query,
    w_key,
    w_value,
    feed_rows,
    g_b_up,
    pen_tile,
    *rest,
):
    *backs, g_weights, short, g_table, g_rows, g_columns, g_turned, upstream = rest
    slot = pl.program_id(0)
    rows, width = resid_grad.shape[1:]
    cols = base.shape[1]
    heads, size = query_part.shape[1:3]
    own = pl.ds(pl.multiple_of(start[0], rows), rows)

    @pl.when(slot == 0)
    def _():
        for ref in (g_turned, g_table, g_rows, g_columns):
            ref[...] = jnp.zeros_like(ref)

    query_wide = query_part[0].astype(F32).reshape(width, rows)
    value_wide = value_part[0].astype(F32).reshape(width, cols)
    query_grad = query_wide.astype(BF16)
    key_grad = key_part[0].astype(F32).reshape(width, cols).astype(BF16)
    value_grad = value_wide.astype(BF16)
    g_turned[0] += dot(query_grad, normed[0, own, :], NN)
    g_turned[1] += dot(key_grad, normed[0], NN)
    g_turned[2] += dot(value_grad, normed[0], NN)
    g_columns[0] += jnp.sum(query_grad.astype(F32), axis=1, keepdims=True)
    g_columns[1] += jnp.sum(value_wide, axis=1, keepdims=True)
    upstream[...] = dot(key_grad, w_key[...], TT) + dot(value_grad, w_value[...], TT)
    upstream[own, :] += dot(query_grad, w_query[...], TT)
    unit, inverse = unit_of(base[0])
    received = upstream[...]
    g_rows[0:1] += column_sum(received * unit)
    g_rows[1:2] += column_sum(received)
    upstream[...] = norm_back(received, unit, inverse, gain[...])
    if len(backs) == 1:
        backs[0][0] = upstream[...]
    else:
        backs[1][0] = upstream[pl.ds(pl.multiple_of(start[1], rows), rows), :].astype(BF16)
    upstream[own, :] += resid_grad[0]
    if len(backs) == 2:
        backs[0][0] = upstream[own, :]
    total = upstream[...]
    upper = total.astype(BF16)
    lower = (total - upper.astype(F32)).astype(BF16)
    onehot = onehot_of(types[0], g_table.shape[0], 1)
    g_table[...] += dot(onehot, upper, NN) + dot(onehot, lower, NN)

    @pl.when(slot == pl.num_programs(0) - 1)
    def _():
        for i in range(3):
            g_weights[i * width : (i + 1) * width] = g_turned[i].T
        lines = [g_table[...], g_rows[...]]
        lines += [jnp.broadcast_to(g_columns[i], (width, 128)).T[:1] for i in range(2)]
        lines += [feed_rows[...]]
        lines += [g_b_up[:, i : i + width] for i in range(0, g_b_up.shape[1], width)]
        lines += [jnp.full((1, width), 0.5 * jnp.sum(pen_tile[...]))]
        at = 0
        short[...] = jnp.zeros_like(short)
        for values in lines:
            short[at : at + values.shape[0]] = values
            at += values.shape[0]


def finish(
    start,
    query_part,
    key_part,
    value_part,
    base,
    normed,
    types,
    resid_grad,
    gain,
    w_query,
    w_key,
    w_value,
    feed_rows,
    g_b_up,
    pen_tile,
    type_count,
    lines,
    halves,
):
    slots, heads, size, rows = query_part.shape
    cols, width = base.shape[1:]
    square = whole((width, width))
    backs = [((rows, width), F32), ((rows, width), BF16)] if halves else [((cols, width), F32)]
    shared = [((3 * width, width), F32), ((lines, width), F32)]
    return pl.pallas_call(
        finish_body,
        grid=(slots,),
        in_specs=[
            pl.BlockSpec(memory_space=pltpu.SMEM),
            by_slot(heads, size, rows),
            by_slot(heads, size, cols),
            by_slot(heads, size, cols),
            by_slot(cols, width),
            by_slot(cols, width),
            by_slot(1, cols),
            by_slot(rows, width),
            whole((1, width)),
            square,
            square,
            square,
            whole(feed_rows.shape),
            whole(g_b_up.shape),
            whole(pen_tile.shape),
        ],
        out_specs=[by_slot(*shape) for shape, _ in backs] + [whole(shape) for shape, _ in shared],
        out_shape=[jax.ShapeDtypeStruct((slots,) + shape, kind) for shape, kind in backs]
        + [jax.ShapeDtypeStruct(shape, kind) for shape, kind in shared],
        scratch_shapes=[
            pltpu.VMEM((type_count, width), F32),
            pltpu.VMEM((2, width), F32),
            pltpu.VMEM((2, width, 1), F32),
            pltpu.VMEM((3, width, width), F32),
            pltpu.VMEM((cols, width), F32),
        ],
        compiler_params=pltpu.CompilerParams(vmem_limit_bytes=56 << 20),
        name="finish",
    )(
        start,
        query_part,
        key_part,
        value_part,
        base,
        normed,
        types,
        resid_grad,
        gain,
        w_query,
        w_key,
        w_value,
        feed_rows,
        g_b_up,
        pen_tile,
    )


def forward_body(
    safe, pf, query, key, value, row_ids, col_ids, mixed, top, mask, bias, kept
):
    slot = pl.program_id(0)
    group = pl.program_id(1)
    heads = pf.shape[1]

    @pl.when(group == 0)
    def _():
        same = upright(row_ids[0]) == col_ids[0].astype(F32)
        mask[...] = jnp.where(same, 1.0, 0.0).astype(BF16)
        bias[...] = jnp.where(same, 0.0, -BIG)

    def logits_of(h):
        return dot(query[0, h], key[0, h], TN) + pf[0, h].astype(F32)

    def weigh(h, spot):
        mixed[0, h] = dot(value[0, h], kept[spot], NT)

    is_safe = safe[slot] == 1

    @pl.when(is_safe)
    def _():
        top[...] = jnp.zeros_like(top)

        for h in range(heads):
            kept[h % 2] = jnp.exp(logits_of(h)).astype(BF16) * mask[...]
            if h:
                weigh(h - 1, (h - 1) % 2)
        weigh(heads - 1, (heads - 1) % 2)

    @pl.when(jnp.logical_not(is_safe))
    def _():
        def block(i, carry):
            for u in range(STEP):
                h = i * STEP + u
                masked = logits_of(h) + bias[...]
                highest = jnp.max(masked, axis=1, keepdims=True)
                top[0, i, :, u : u + 1] = highest
                kept[0] = jnp.exp(masked - highest).astype(BF16)
                weigh(h, 0)
            return carry

        lax.fori_loop(0, heads // STEP, block, 0)


def attend(safe, pf, query, key, value, row_ids, col_ids, per_step):
    slots, heads, rows, cols = pf.shape

    def by_head(height, width):
        return pl.BlockSpec((1, per_step, height, width), lambda s, g: (s, g, 0, 0))

    return pl.pallas_call(
        forward_body,
        grid=(slots, heads // per_step),
        in_specs=[
            pl.BlockSpec(memory_space=pltpu.SMEM),
            by_head(rows, cols),
            by_head(16, rows),
            by_head(16, cols),
            by_head(16, cols),
            pl.BlockSpec((1, 1, rows), lambda s, g: (s, 0, 0)),
            pl.BlockSpec((1, 1, cols), lambda s, g: (s, 0, 0)),
        ],
        out_specs=[
            by_head(16, rows),
            pl.BlockSpec((1, per_step // STEP, rows, STEP), lambda s, g: (s, g, 0, 0)),
        ],
        out_shape=[
            jax.ShapeDtypeStruct((slots, heads, 16, rows), F32),
            jax.ShapeDtypeStruct((slots, heads // STEP, rows, STEP), F32),
        ],
        scratch_shapes=[
            pltpu.VMEM((rows, cols), BF16),
            pltpu.VMEM((rows, cols), F32),
            pltpu.VMEM((2, rows, cols), BF16),
        ],
        compiler_params=pltpu.CompilerParams(vmem_limit_bytes=56 << 20),
        name="attend",
    )(safe, pf, query, key, value, row_ids, col_ids)


def backward_body(
    safe,
    scale,
    pf,
    cotan,
    query,
    key,
    grad,
    value,
    log_total,
    row_ids,
    col_ids,
    pair_out,
    pair_grad,
    query_grad,
    key_grad,
    value_grad,
    penalty,
    weight,
    mask,
    bias,
    probs,
):
    slot = pl.program_id(0)
    group = pl.program_id(1)
    heads = pf.shape[1]
    rows, cols = pf.shape[2:]

    @pl.when(group == 0)
    def _():
        same = upright(row_ids[0]) == col_ids[0].astype(F32)
        weight[...] = jnp.where(same, scale[0], 0.0).astype(BF16)
        mask[...] = jnp.where(same, 1.0, 0.0).astype(BF16)
        bias[...] = jnp.where(same, 0.0, -BIG)

    @pl.when((group == 0) & (slot == 0))
    def _():
        penalty[...] = jnp.zeros_like(penalty)

    def pairs(i, u, safe):
        h = i * STEP + u
        logits = dot(query[0, h], key[0, h], TN) + pf[0, h].astype(F32)
        logits_low = logits.astype(BF16)
        pair_out[0, h] = logits_low
        probs_grad = dot(grad[0, h], value[0, h], TN).astype(BF16)
        shifted = logits - log_total[0, i, :, u : u + 1]
        if safe:
            prob = jnp.exp(shifted).astype(BF16) * mask[...]
        else:
            prob = jnp.exp(shifted + bias[...]).astype(BF16)
        probs[h % 2] = prob
        pen_grad = logits_low * weight[...]
        pair_grad[0, h] = prob * probs_grad + (cotan[0, h] + pen_grad)
        squares = pen_grad * logits_low
        while squares.shape[0] > 16:
            half = squares.shape[0] // 2
            squares = squares[:half] + squares[half:]
        penalty[...] += squares.astype(F32)

    def sums(h, spot):
        upper = dot(query[0, h], pair_grad[0, h], NN)
        key_grad[0, h] = (upper[:8] + upper[8:]).astype(BF16)
        value_grad[0, h] = dot(grad[0, h], probs[spot], NN)[:8].astype(BF16)
        query_grad[0, h] = (dot(key[0, h], pair_grad[0, h], NT)[:8] * 8**-0.5).astype(BF16)

    is_safe = safe[slot] == 1

    @pl.when(is_safe)
    def _():
        for h in range(heads):
            pairs(h // STEP, h % STEP, True)
            if h:
                sums(h - 1, (h - 1) % 2)
        sums(heads - 1, (heads - 1) % 2)

    @pl.when(jnp.logical_not(is_safe))
    def _():
        for h in range(heads):
            pairs(h // STEP, h % STEP, False)
            sums(h, h % 2)


def attend_back(
    safe, scale, pf, cotan, query, key, grad, value, log_total, row_ids, col_ids, per_step
):
    slots, heads, rows, cols = pf.shape

    def by_head(height, width):
        return pl.BlockSpec((1, per_step, height, width), lambda s, g: (s, g, 0, 0))

    return pl.pallas_call(
        backward_body,
        grid=(slots, heads // per_step),
        in_specs=[
            pl.BlockSpec(memory_space=pltpu.SMEM),
            pl.BlockSpec(memory_space=pltpu.SMEM),
            by_head(rows, cols),
            by_head(rows, cols),
            by_head(16, rows),
            by_head(16, cols),
            by_head(16, rows),
            by_head(16, cols),
            pl.BlockSpec((1, per_step // STEP, rows, STEP), lambda s, g: (s, g, 0, 0)),
            pl.BlockSpec((1, 1, rows), lambda s, g: (s, 0, 0)),
            pl.BlockSpec((1, 1, cols), lambda s, g: (s, 0, 0)),
        ],
        out_specs=[
            by_head(rows, cols),
            by_head(rows, cols),
            by_head(8, rows),
            by_head(8, cols),
            by_head(8, cols),
            pl.BlockSpec((16, cols), lambda s, g: (0, 0)),
        ],
        out_shape=[
            jax.ShapeDtypeStruct((slots, heads, rows, cols), BF16),
            jax.ShapeDtypeStruct((slots, heads, rows, cols), BF16),
            jax.ShapeDtypeStruct((slots, heads, 8, rows), BF16),
            jax.ShapeDtypeStruct((slots, heads, 8, cols), BF16),
            jax.ShapeDtypeStruct((slots, heads, 8, cols), BF16),
            jax.ShapeDtypeStruct((16, cols), F32),
        ],
        scratch_shapes=[
            pltpu.VMEM((rows, cols), BF16),
            pltpu.VMEM((rows, cols), BF16),
            pltpu.VMEM((rows, cols), F32),
            pltpu.VMEM((2, rows, cols), BF16),
        ],
        compiler_params=pltpu.CompilerParams(vmem_limit_bytes=60 << 20),
        name="attend_back",
    )(safe, scale, pf, cotan, query, key, grad, value, log_total, row_ids, col_ids)


def flips(sizes):
    found = []
    for axis in ("slot", "blk"):
        bit = 1
        while bit < sizes[axis]:
            found.append((axis, bit))
            bit *= 2
    return found


def swap(values, sizes, axis, bit):
    return lax.ppermute(values, axis, [(i, i ^ bit) for i in range(sizes[axis])])


def butterfly(values, sizes, axes=("slot", "blk")):
    for axis, bit in flips(sizes):
        if axis in axes:
            values = values + swap(values, sizes, axis, bit)
    return values


def step_plan(sizes):
    whole = sizes["slot"] * sizes["blk"]
    blk = sizes["blk"]
    slot_at = lax.axis_index("slot")
    blk_at = lax.axis_index("blk")

    def partner(device, axis, bit):
        s, b = divmod(device, blk)
        return (s ^ bit) * blk + b if axis == "slot" else s * blk + (b ^ bit)

    def bit_of(axis, bit):
        return ((slot_at if axis == "slot" else blk_at) // bit) % 2

    def plain(axis, bit):
        return ([(d, partner(d, axis, bit)) for d in range(whole)], bit_of(axis, bit))

    def mixed(even, odd):
        pairs = [(d, partner(d, *(even if (d // blk) % 2 == 0 else odd))) for d in range(whole)]
        return (pairs, jnp.where(slot_at % 2 == 0, bit_of(*even), bit_of(*odd)))

    steps = flips(sizes)
    core, rest = steps[0], steps[1:]
    near_y, near_x = ("slot", 2), ("blk", 1)
    plan = [plain(*core)]
    if near_y in rest and near_x in rest:
        rest = [step for step in rest if step not in (near_y, near_x)]
        plan += [mixed(near_x, near_y), mixed(near_y, near_x)]
    return plan + [plain(*step) for step in rest]


def sum_all(wide, small, plan):
    joint = ("slot", "blk")
    rows, extra = wide.shape[1], small.shape[1]

    def parcel(wide, small):
        upper = rounded(small)
        parts = [wide.astype(BF16), upper.astype(BF16), (small - upper).astype(BF16)]
        return jnp.concatenate(parts, 1)

    def unpack(values):
        values = values.astype(F32)
        return values[:, :rows], values[:, rows : rows + extra] + values[:, rows + extra :]

    def pick(values, half):
        halves = values.reshape((2, values.shape[0] // 2) + values.shape[1:])
        return lax.dynamic_index_in_dim(halves, half, 0, keepdims=False)

    for pairs, half in plan:
        away = parcel(pick(wide, 1 - half), pick(small, 1 - half))
        came_wide, came_small = unpack(lax.ppermute(away, joint, pairs))
        wide = pick(wide, half) + came_wide
        small = pick(small, half) + came_small
    values = parcel(wide, small)
    for pairs, half in plan[::-1]:
        came = lax.ppermute(values, joint, pairs)
        values = jnp.where(
            half == 0,
            jnp.concatenate([values, came], 0),
            jnp.concatenate([came, values], 0),
        )
    return unpack(values)


def sum_wide(values, sizes, after):
    joint = ("slot", "blk")
    count = sizes["slot"] * sizes["blk"]
    terms = lax.all_to_all(values, joint, 0, 0, tiled=True)
    terms, after = lax.optimization_barrier((terms, after))
    terms = terms.reshape((count, values.shape[0] // count, values.shape[1]))
    total = jnp.sum(terms.astype(F32), axis=0).astype(BF16)
    return lax.all_gather(total, joint, tiled=True), after


def local(
    sizes,
    atom_feats,
    pair_feats,
    type_ids,
    mol_lengths,
    type_table,
    ln1_gain,
    ln1_shift,
    w_query,
    b_query,
    w_key,
    w_value,
    b_value,
    w_out,
    b_out,
    ln2_gain,
    ln2_shift,
    w_up,
    b_up,
    w_down,
    b_down,
    atom_cotan,
    pair_cotan,
):
    slots, rows, width = atom_feats.shape
    heads = pair_feats.shape[1]
    cols = pair_feats.shape[3]
    types = type_table.shape[0]
    blk_at = lax.axis_index("blk")
    row_start = blk_at * rows
    plan = step_plan(sizes)

    def own(values, axis=1):
        return lax.dynamic_slice_in_dim(values, row_start, rows, axis)

    bounds = jnp.cumsum(mol_lengths, axis=1)
    places = jnp.arange(cols, dtype=jnp.int32)
    mol_ids = jnp.sum((places[None, :, None] >= bounds[:, None, :]).astype(jnp.int32), axis=2)
    row_mols = own(mol_ids)
    row_ids = row_mols[:, None, :]
    col_ids = mol_ids[:, None, :]

    first = rounded(type_table)
    second = rounded(type_table - first)
    table = jnp.concatenate([first, second, type_table - first - second], 0).astype(BF16)
    start = row_start.astype(jnp.int32).reshape(1)
    here = blk_at.astype(jnp.int32).reshape(1)

    def line(values):
        return values.reshape(1, -1)

    shared = (table, line(ln1_gain), line(ln1_shift), w_key, w_value, line(b_value))
    asking = (w_query, line(b_query))

    def safe_of(reach):
        furthest = (width // heads) ** (-0.5) * jnp.sqrt(reach[:, 0, 0]) + PAIR_LIMIT
        return (furthest <= SAFE_LOGIT).astype(jnp.int32)

    count = jnp.sum(mol_lengths * mol_lengths).astype(F32).reshape(1, 1)
    if sizes["blk"] == 2:
        there = 1 - here
        came_feats = swap(atom_feats, sizes, "blk", 1)
        came_types = swap(type_ids, sizes, "blk", 1)
        near = [swap(count, sizes, "slot", bit) for bit in (1, 2, 3)]
        base, normed, key_rows, value_rows, reach, far_query, query_rows = prepare(
            here,
            jnp.zeros((1,), jnp.int32),
            atom_feats,
            type_ids[:, None, :],
            shared,
            heads,
            rows,
            cols,
            asking,
        )
        safe = safe_of(reach)
        near, reach = lax.optimization_barrier((near, reach))
        count = count + near[0] + (near[1] + near[2])
        far = [swap(count, sizes, "slot", bit) for bit in range(4, sizes["slot"], 4)]
        base, normed, key_rows, value_rows, reach = prepare(
            there,
            start,
            came_feats,
            came_types[:, None, :],
            shared,
            heads,
            rows,
            cols,
            (far_query, base, normed, key_rows, value_rows),
        )
        safe = safe * safe_of(reach)
        far, safe = lax.optimization_barrier((far, safe))
        pair_total = count + sum(far)
        all_types = jnp.where(
            blk_at == 0,
            jnp.concatenate([type_ids, came_types], 1),
            jnp.concatenate([came_types, type_ids], 1),
        )
    else:
        feats = lax.all_gather(atom_feats, "blk", axis=1, tiled=True)
        all_types = lax.all_gather(type_ids, "blk", axis=1, tiled=True)
        zero = jnp.zeros((1,), jnp.int32)
        base, normed, key_rows, value_rows, reach, _, query_rows = prepare(
            zero,
            start,
            feats,
            all_types[:, None, :],
            shared,
            heads,
            rows,
            cols,
            asking,
        )
        safe = safe_of(reach)
        pair_total = butterfly(count, sizes, ("slot",))
    pen_scale = (2.0 / pair_total).reshape(1)
    weighed, top = attend(
        safe, pair_feats, query_rows, key_rows, value_rows, row_ids, col_ids, 32
    )
    types_row = all_types[:, None, :]

    atom_out, grad_rows, log_total, resid_grad, g_feed, g_b_up, feed_rows = feed(
        here,
        top,
        weighed,
        base,
        atom_cotan,
        w_out,
        line(b_out),
        line(ln2_gain),
        line(ln2_shift),
        w_up,
        line(b_up),
        w_down,
        line(b_down),
    )

    pair_out, pair_grad, query_part, key_part, value_part, pen_tile = attend_back(
        safe,
        pen_scale,
        pair_feats,
        pair_cotan,
        query_rows,
        key_rows,
        grad_rows,
        value_rows,
        log_total,
        row_ids,
        col_ids,
        16,
    )

    devices = sizes["slot"] * sizes["blk"]
    used = types + 9 + g_b_up.shape[1] // width
    halves = sizes["blk"] == 2
    *backs, g_weights, short = finish(
        jnp.concatenate([start, rows - start]),
        query_part,
        key_part,
        value_part,
        base,
        normed,
        types_row,
        resid_grad,
        line(ln1_gain),
        w_query,
        w_key,
        w_value,
        feed_rows,
        g_b_up,
        pen_tile,
        types,
        used + -used % devices,
        halves,
    )
    g_feed, short = sum_wide(g_feed, sizes, short)
    if halves:
        base_grad = backs[0] + swap(backs[1], sizes, "blk", 1).astype(F32)
    else:
        base_grad = resid_grad + lax.psum_scatter(backs[0], "blk", scatter_dimension=1, tiled=True)
    hidden = w_up.shape[1]
    g_w_up = jnp.concatenate(
        [g_feed[at : at + width] for at in range(hidden + width, 2 * hidden + width, width)], 1
    ).astype(F32)
    g_w_down = g_feed[:hidden].astype(F32)
    g_w_out = g_feed[hidden : hidden + width].astype(F32)
    g_weights, packed = sum_all(
        g_weights.reshape(devices, -1, width), short.reshape(devices, -1, width), plan
    )
    g_weights = g_weights.reshape(3 * width, width)
    packed = packed.reshape(-1, width)[:used]
    at = types
    (
        g_ln1_gain,
        g_ln1_shift,
        g_b_query,
        g_b_value,
        g_b_out,
        g_ln2_gain,
        g_ln2_shift,
        g_b_down,
    ) = (packed[at + i] for i in range(8))
    return (
        atom_out,
        pair_out,
        packed[-1, 0],
        base_grad.astype(BF16),
        pair_grad,
        packed[:types],
        g_ln1_gain,
        g_ln1_shift,
        g_weights[:width],
        g_b_query,
        g_weights[width : 2 * width],
        g_weights[2 * width :],
        g_b_value,
        g_w_out,
        g_b_out,
        g_ln2_gain,
        g_ln2_shift,
        g_w_up,
        packed[at + 8 : used - 1].reshape(-1),
        g_w_down,
        g_b_down,
    )


def solution(mesh):
    atoms = P("slot", "blk", None)
    pairs = P("slot", None, "blk", None)
    sizes = {axis: mesh.shape[axis] for axis in ("slot", "blk")}
    return jax.shard_map(
        functools.partial(local, sizes),
        mesh=mesh,
        in_specs=(atoms, pairs, P("slot", "blk"), P("slot", None))
        + (P(),) * 16
        + (atoms, pairs),
        out_specs=(atoms, pairs, P(), atoms, pairs) + (P(),) * 16,
        check_vma=False,
    )
```

```python
import functools

import jax
import jax.numpy as jnp
from jax import lax
from jax.experimental import pallas as pl
from jax.experimental.pallas import tpu as pltpu
from jax.sharding import PartitionSpec as P

EPSILON = 1e-05
F32 = jnp.float32
BF16 = jnp.bfloat16
BIG = 1073741824.0
TN = (((0,), (0,)), ((), ()))
NT = (((1,), (1,)), ((), ()))
NN = (((1,), (0,)), ((), ()))
TT = (((0,), (1,)), ((), ()))
STEP = 8
CHUNK = 512
PAIR_LIMIT = 6.0
SAFE_LOGIT = 40.0


def dot(left, right, dims):
    return lax.dot_general(left, right, dims, preferred_element_type=F32)


def rounded(values):
    return lax.reduce_precision(values, 8, 7)


def unit_of(values):
    center = values - jnp.mean(values, axis=-1, keepdims=True)
    inverse = lax.rsqrt(jnp.mean(center * center, axis=-1, keepdims=True) + EPSILON)
    return center * inverse, inverse


def norm_back(upstream, unit, inverse, gain):
    scaled = upstream * gain
    first = jnp.mean(scaled, axis=-1, keepdims=True)
    second = jnp.mean(scaled * unit, axis=-1, keepdims=True)
    return inverse * (scaled - first - unit * second)


def column_sum(values):
    return jnp.sum(values, axis=0, keepdims=True)


def onehot_of(ids, types, copies):
    line = lax.broadcasted_iota(jnp.int32, (types * copies, ids.shape[1]), 0)
    hit = line == ids
    for i in range(1, copies):
        hit = hit | (line == ids + i * types)
    return jnp.where(hit, 1.0, 0.0).astype(BF16)


def upright(values):
    return jnp.broadcast_to(values.astype(F32), (8, values.shape[1])).T[:, :1]


def whole(shape):
    return pl.BlockSpec(shape, lambda *grid: (0,) * len(shape))


def by_slot(*shape):
    return pl.BlockSpec((1,) + shape, lambda s: (s,) + (0,) * len(shape))


def prepare_body(first, at, start, *refs):
    feats, types, table, gain, shift, w_key, w_value, b_value = refs[:8]
    if first:
        w_query, b_query = refs[8:10]
        base_out, normed_out, key_out, value_out, reach, far_out, query_out = refs[10:]
    else:
        far_query = refs[8]
        base_out, normed_out, key_out, value_out, reach = refs[13:]
    heads, _, cols = key_out.shape[1:]
    width = feats.shape[2]
    size = width // heads
    base = feats[0].astype(F32) + dot(
        onehot_of(types[0], table.shape[0] // 3, 3), table[...], TN
    )
    base_out[0] = base
    unit, _ = unit_of(base)
    normed = (unit * gain[...] + shift[...]).astype(BF16)
    normed_out[0] = normed

    def split_heads(values):
        return values.reshape(heads, size, values.shape[1])

    def far(values):
        return jnp.max(jnp.sum(values * values, axis=1), axis=1, keepdims=True)

    key = split_heads(dot(w_key[...], normed, TT).astype(BF16).astype(F32))
    key_out[0] = jnp.concatenate([key, key], 1).astype(BF16)
    value = split_heads(dot(w_value[...], normed, TT) + upright(b_value[...]))
    line = lax.broadcasted_iota(jnp.int32, (heads, size, cols), 1)
    value_out[0] = jnp.concatenate([value, jnp.where(line < 3, 1.0, 0.0)], 1).astype(BF16)
    if first:
        rows = query_out.shape[3]
        own = normed_out[0, pl.ds(pl.multiple_of(start[0], rows), rows), :]
        query = split_heads((dot(w_query[...], own, TT) + upright(b_query[...])).astype(BF16).astype(F32))
        scaled = query * size ** (-0.5)
        upper = scaled.astype(BF16).astype(F32)
        query_out[0] = jnp.concatenate([upper, scaled - upper], 1).astype(BF16)
        furthest = jnp.broadcast_to(far(query), far_out.shape[1:])
        far_out[0] = furthest
    else:
        furthest = far_query[0]
    reach[0] = jnp.broadcast_to(jnp.max(furthest * far(key)), reach.shape[1:])


def prepare(at, start, feats, types, shared, heads, rows, cols, extra):
    slots, part, width = feats.shape
    first = len(extra) == 2
    square = whole((width, width))
    row = whole((1, width))

    def across(s, at, start):
        return (s, at[0], 0)

    def along(s, at, start):
        return (s, 0, 0, at[0])

    def fixed(*shape):
        return pl.BlockSpec((1,) + shape, lambda s, at, start: (s,) + (0,) * len(shape))

    kept = pl.BlockSpec(memory_space=pl.ANY)
    outs = [
        ((cols, width), F32, pl.BlockSpec((1, part, width), across)),
        ((cols, width), BF16, pl.BlockSpec((1, part, width), across)),
        ((heads, 16, cols), BF16, pl.BlockSpec((1, heads, 16, part), along)),
        ((heads, 16, cols), BF16, pl.BlockSpec((1, heads, 16, part), along)),
        ((8, 128), F32, fixed(8, 128)),
    ]
    if first:
        outs.append(((heads, 128), F32, fixed(heads, 128)))
        outs.append(((heads, 16, rows), BF16, fixed(heads, 16, rows)))
    return pl.pallas_call(
        functools.partial(prepare_body, first),
        grid_spec=pltpu.PrefetchScalarGridSpec(
            num_scalar_prefetch=2,
            grid=(slots,),
            in_specs=[
                fixed(part, width),
                fixed(1, part),
                whole(shared[0].shape),
                row,
                row,
                square,
                square,
                row,
            ]
            + ([square, row] if first else [fixed(heads, 128)] + [kept] * 4),
            out_specs=[spec for _, _, spec in outs],
        ),
        out_shape=[jax.ShapeDtypeStruct((slots,) + shape, kind) for shape, kind, _ in outs],
        input_output_aliases={} if first else {11 + i: i for i in range(4)},
        compiler_params=pltpu.CompilerParams(vmem_limit_bytes=40 << 20),
        name="prepare",
    )(at, start, feats, types, *shared, *extra)


def feed_body(
    at,
    top,
    weighed,
    base,
    cotan,
    w_out,
    b_out,
    gain,
    shift,
    w_up,
    b_up,
    w_down,
    b_down,
    atom_out,
    grad_rows,
    log_total,
    resid_grad_out,
    g_weights,
    g_b_up,
    g_rows,
    total,
):
    slot = pl.program_id(0)
    heads, _, rows = weighed.shape[1:]
    width = base.shape[2]
    size = width // heads
    hidden_width = w_up.shape[1]

    @pl.when(slot == 0)
    def _():
        for ref in (total, g_b_up, g_rows):
            ref[...] = jnp.zeros_like(ref)

    totals = weighed[0, :, size : size + 1, :]
    mixed = weighed[0, :, :size, :] / totals
    logs = jnp.log(totals).reshape(heads, rows)
    for g in range(heads // STEP):
        log_total[0, g] = top[0, g] + logs[g * STEP : (g + 1) * STEP].T
    mixed_low = mixed.reshape(width, rows).astype(BF16)
    resid = base[0] + dot(mixed_low, w_out[...], TN) + b_out[...]
    unit, inverse = unit_of(resid)
    normed = (unit * gain[...] + shift[...]).astype(BF16)
    grad = cotan[0]
    down = jnp.zeros((rows, width), F32)
    back = jnp.zeros((rows, width), F32)
    for at in range(0, hidden_width, CHUNK):
        part = slice(at, at + CHUNK)
        pre = dot(normed, w_up[:, part], NN) + b_up[:, part]
        cumulative = 0.5 * (1.0 + lax.erf(pre * 0.7071067811865476))
        density = jnp.exp(-0.5 * pre * pre) * 0.3989422804014327
        hidden = (pre * cumulative).astype(BF16)
        down += dot(hidden, w_down[part, :], NN)
        total[part, :] += dot(hidden, grad, TN)
        hidden_grad = (
            dot(grad, w_down[part, :], NT) * (cumulative + pre * density)
        ).astype(BF16)
        back += dot(hidden_grad, w_up[:, part], NT)
        total[hidden_width + width + at : hidden_width + 2 * width + at] += dot(
            normed, hidden_grad, TN
        )
        g_b_up[:, part] += column_sum(hidden_grad.astype(F32))
    atom_out[0] = (resid + down + b_down[...]).astype(BF16)
    resid_grad = grad.astype(F32) + norm_back(back, unit, inverse, gain[...])
    resid_grad_out[0] = resid_grad
    low = resid_grad.astype(BF16)
    total[hidden_width : hidden_width + width] += dot(mixed_low, low, NN)
    g_rows[0:1] += column_sum(low.astype(F32))
    g_rows[1:2] += column_sum(back * unit)
    g_rows[2:3] += column_sum(back)
    g_rows[3:4] += column_sum(grad.astype(F32))
    mixed_grad = dot(w_out[...], low, NT).astype(BF16).astype(F32).reshape(heads, size, rows)
    delta = -jnp.sum(mixed_grad * mixed, axis=1, keepdims=True)
    first = delta.astype(BF16).astype(F32)
    second = (delta - first).astype(BF16).astype(F32)
    line = lax.broadcasted_iota(jnp.int32, (heads, size, rows), 1)
    extra = jnp.where(
        line == 0,
        first,
        jnp.where(line == 1, second, jnp.where(line == 2, delta - first - second, 0.0)),
    )
    grad_rows[0] = jnp.concatenate([mixed_grad, extra], 1).astype(BF16)

    @pl.when(slot == pl.num_programs(0) - 1)
    def _():
        g_weights[...] = total[...].astype(BF16)


def feed(at, top, weighed, base, cotan, w_out, b_out, gain, shift, w_up, b_up, w_down, b_down):
    slots, heads, _, rows = weighed.shape
    width, hidden = w_up.shape
    row = whole((1, width))
    own = [
        ((rows, width), BF16),
        ((heads, 16, rows), BF16),
        ((heads // STEP, rows, STEP), F32),
        ((rows, width), F32),
    ]
    shared = [
        ((2 * hidden + width, width), BF16),
        ((1, hidden), F32),
        ((4, width), F32),
    ]

    def by_slot(*shape):
        return pl.BlockSpec((1,) + shape, lambda s, at: (s,) + (0,) * len(shape))

    return pl.pallas_call(
        feed_body,
        grid_spec=pltpu.PrefetchScalarGridSpec(
            num_scalar_prefetch=1,
            grid=(slots,),
            in_specs=[
                by_slot(heads // STEP, rows, STEP),
                by_slot(heads, 16, rows),
                pl.BlockSpec((1, rows, width), lambda s, at: (s, at[0], 0)),
            by_slot(rows, width),
            whole((width, width)),
            row,
            row,
            row,
            whole((width, hidden)),
            whole((1, hidden)),
            whole((hidden, width)),
            row,
        ],
        out_specs=[by_slot(*shape) for shape, _ in own] + [whole(shape) for shape, _ in shared],
            scratch_shapes=[pltpu.VMEM(shared[0][0], F32)],
        ),
        out_shape=[jax.ShapeDtypeStruct((slots,) + shape, kind) for shape, kind in own]
        + [jax.ShapeDtypeStruct(shape, kind) for shape, kind in shared],
        compiler_params=pltpu.CompilerParams(vmem_limit_bytes=52 << 20),
        name="feed",
    )(at, top, weighed, base, cotan, w_out, b_out, gain, shift, w_up, b_up, w_down, b_down)


def finish_body(
    start,
    query_part,
    key_part,
    value_part,
    base,
    normed,
    types,
    resid_grad,
    gain,
    w_query,
    w_key,
    w_value,
    feed_rows,
    g_b_up,
    pen_tile,
    *rest,
):
    *backs, g_weights, short, g_table, g_rows, g_columns, g_turned, upstream = rest
    slot = pl.program_id(0)
    rows, width = resid_grad.shape[1:]
    cols = base.shape[1]
    heads, size = query_part.shape[1:3]
    own = pl.ds(pl.multiple_of(start[0], rows), rows)

    @pl.when(slot == 0)
    def _():
        for ref in (g_turned, g_table, g_rows, g_columns):
            ref[...] = jnp.zeros_like(ref)

    query_wide = query_part[0].astype(F32).reshape(width, rows)
    value_wide = value_part[0].astype(F32).reshape(width, cols)
    query_grad = query_wide.astype(BF16)
    key_grad = key_part[0].astype(F32).reshape(width, cols).astype(BF16)
    value_grad = value_wide.astype(BF16)
    g_turned[0] += dot(query_grad, normed[0, own, :], NN)
    g_turned[1] += dot(key_grad, normed[0], NN)
    g_turned[2] += dot(value_grad, normed[0], NN)
    g_columns[0] += jnp.sum(query_grad.astype(F32), axis=1, keepdims=True)
    g_columns[1] += jnp.sum(value_wide, axis=1, keepdims=True)
    upstream[...] = dot(key_grad, w_key[...], TT) + dot(value_grad, w_value[...], TT)
    upstream[own, :] += dot(query_grad, w_query[...], TT)
    unit, inverse = unit_of(base[0])
    received = upstream[...]
    g_rows[0:1] += column_sum(received * unit)
    g_rows[1:2] += column_sum(received)
    upstream[...] = norm_back(received, unit, inverse, gain[...])
    if len(backs) == 1:
        backs[0][0] = upstream[...]
    else:
        backs[1][0] = upstream[pl.ds(pl.multiple_of(start[1], rows), rows), :].astype(BF16)
    upstream[own, :] += resid_grad[0]
    if len(backs) == 2:
        backs[0][0] = upstream[own, :]
    total = upstream[...]
    upper = total.astype(BF16)
    lower = (total - upper.astype(F32)).astype(BF16)
    onehot = onehot_of(types[0], g_table.shape[0], 1)
    g_table[...] += dot(onehot, upper, NN) + dot(onehot, lower, NN)

    @pl.when(slot == pl.num_programs(0) - 1)
    def _():
        for i in range(3):
            g_weights[i * width : (i + 1) * width] = g_turned[i].T
        lines = [g_table[...], g_rows[...]]
        lines += [jnp.broadcast_to(g_columns[i], (width, 128)).T[:1] for i in range(2)]
        lines += [feed_rows[...]]
        lines += [g_b_up[:, i : i + width] for i in range(0, g_b_up.shape[1], width)]
        lines += [jnp.full((1, width), 0.5 * jnp.sum(pen_tile[...]))]
        at = 0
        short[...] = jnp.zeros_like(short)
        for values in lines:
            short[at : at + values.shape[0]] = values
            at += values.shape[0]


def finish(
    start,
    query_part,
    key_part,
    value_part,
    base,
    normed,
    types,
    resid_grad,
    gain,
    w_query,
    w_key,
    w_value,
    feed_rows,
    g_b_up,
    pen_tile,
    type_count,
    lines,
    halves,
):
    slots, heads, size, rows = query_part.shape
    cols, width = base.shape[1:]
    square = whole((width, width))
    backs = [((rows, width), F32), ((rows, width), BF16)] if halves else [((cols, width), F32)]
    shared = [((3 * width, width), F32), ((lines, width), F32)]
    return pl.pallas_call(
        finish_body,
        grid=(slots,),
        in_specs=[
            pl.BlockSpec(memory_space=pltpu.SMEM),
            by_slot(heads, size, rows),
            by_slot(heads, size, cols),
            by_slot(heads, size, cols),
            by_slot(cols, width),
            by_slot(cols, width),
            by_slot(1, cols),
            by_slot(rows, width),
            whole((1, width)),
            square,
            square,
            square,
            whole(feed_rows.shape),
            whole(g_b_up.shape),
            whole(pen_tile.shape),
        ],
        out_specs=[by_slot(*shape) for shape, _ in backs] + [whole(shape) for shape, _ in shared],
        out_shape=[jax.ShapeDtypeStruct((slots,) + shape, kind) for shape, kind in backs]
        + [jax.ShapeDtypeStruct(shape, kind) for shape, kind in shared],
        scratch_shapes=[
            pltpu.VMEM((type_count, width), F32),
            pltpu.VMEM((2, width), F32),
            pltpu.VMEM((2, width, 1), F32),
            pltpu.VMEM((3, width, width), F32),
            pltpu.VMEM((cols, width), F32),
        ],
        compiler_params=pltpu.CompilerParams(vmem_limit_bytes=40 << 20),
        name="finish",
    )(
        start,
        query_part,
        key_part,
        value_part,
        base,
        normed,
        types,
        resid_grad,
        gain,
        w_query,
        w_key,
        w_value,
        feed_rows,
        g_b_up,
        pen_tile,
    )


def forward_body(
    safe, pf, query, key, value, row_ids, col_ids, mixed, top, mask, bias, kept
):
    slot = pl.program_id(0)
    group = pl.program_id(1)
    heads = pf.shape[1]

    @pl.when(group == 0)
    def _():
        same = upright(row_ids[0]) == col_ids[0].astype(F32)
        mask[...] = jnp.where(same, 1.0, 0.0).astype(BF16)
        bias[...] = jnp.where(same, 0.0, -BIG)

    def logits_of(h):
        return dot(query[0, h], key[0, h], TN) + pf[0, h].astype(F32)

    def weigh(h, spot):
        mixed[0, h] = dot(value[0, h], kept[spot], NT)

    is_safe = safe[slot] == 1

    @pl.when(is_safe)
    def _():
        top[...] = jnp.zeros_like(top)

        for h in range(heads):
            kept[h % 2] = jnp.exp(logits_of(h)).astype(BF16) * mask[...]
            if h:
                weigh(h - 1, (h - 1) % 2)
        weigh(heads - 1, (heads - 1) % 2)

    @pl.when(jnp.logical_not(is_safe))
    def _():
        def block(i, carry):
            for u in range(STEP):
                h = i * STEP + u
                masked = logits_of(h) + bias[...]
                highest = jnp.max(masked, axis=1, keepdims=True)
                top[0, i, :, u : u + 1] = highest
                kept[0] = jnp.exp(masked - highest).astype(BF16)
                weigh(h, 0)
            return carry

        lax.fori_loop(0, heads // STEP, block, 0)


def attend(safe, pf, query, key, value, row_ids, col_ids, per_step):
    slots, heads, rows, cols = pf.shape

    def by_head(height, width):
        return pl.BlockSpec((1, per_step, height, width), lambda s, g: (s, g, 0, 0))

    return pl.pallas_call(
        forward_body,
        grid=(slots, heads // per_step),
        in_specs=[
            pl.BlockSpec(memory_space=pltpu.SMEM),
            by_head(rows, cols),
            by_head(16, rows),
            by_head(16, cols),
            by_head(16, cols),
            pl.BlockSpec((1, 1, rows), lambda s, g: (s, 0, 0)),
            pl.BlockSpec((1, 1, cols), lambda s, g: (s, 0, 0)),
        ],
        out_specs=[
            by_head(16, rows),
            pl.BlockSpec((1, per_step // STEP, rows, STEP), lambda s, g: (s, g, 0, 0)),
        ],
        out_shape=[
            jax.ShapeDtypeStruct((slots, heads, 16, rows), F32),
            jax.ShapeDtypeStruct((slots, heads // STEP, rows, STEP), F32),
        ],
        scratch_shapes=[
            pltpu.VMEM((rows, cols), BF16),
            pltpu.VMEM((rows, cols), F32),
            pltpu.VMEM((2, rows, cols), BF16),
        ],
        compiler_params=pltpu.CompilerParams(vmem_limit_bytes=40 << 20),
        name="attend",
    )(safe, pf, query, key, value, row_ids, col_ids)


def backward_body(
    safe,
    scale,
    pf,
    cotan,
    query,
    key,
    grad,
    value,
    log_total,
    row_ids,
    col_ids,
    pair_out,
    pair_grad,
    query_grad,
    key_grad,
    value_grad,
    penalty,
    weight,
    mask,
    bias,
    probs,
):
    slot = pl.program_id(0)
    group = pl.program_id(1)
    heads = pf.shape[1]
    rows, cols = pf.shape[2:]

    @pl.when(group == 0)
    def _():
        same = upright(row_ids[0]) == col_ids[0].astype(F32)
        weight[...] = jnp.where(same, scale[0], 0.0).astype(BF16)
        mask[...] = jnp.where(same, 1.0, 0.0).astype(BF16)
        bias[...] = jnp.where(same, 0.0, -BIG)

    @pl.when((group == 0) & (slot == 0))
    def _():
        penalty[...] = jnp.zeros_like(penalty)

    def pairs(i, u, safe):
        h = i * STEP + u
        logits = dot(query[0, h], key[0, h], TN) + pf[0, h].astype(F32)
        logits_low = logits.astype(BF16)
        pair_out[0, h] = logits_low
        probs_grad = dot(grad[0, h], value[0, h], TN).astype(BF16)
        shifted = logits - log_total[0, i, :, u : u + 1]
        if safe:
            prob = jnp.exp(shifted).astype(BF16) * mask[...]
        else:
            prob = jnp.exp(shifted + bias[...]).astype(BF16)
        probs[h % 2] = prob
        pen_grad = logits_low * weight[...]
        pair_grad[0, h] = prob * probs_grad + (cotan[0, h] + pen_grad)
        squares = pen_grad * logits_low
        while squares.shape[0] > 16:
            half = squares.shape[0] // 2
            squares = squares[:half] + squares[half:]
        penalty[...] += squares.astype(F32)

    def sums(h, spot):
        upper = dot(query[0, h], pair_grad[0, h], NN)
        key_grad[0, h] = (upper[:8] + upper[8:]).astype(BF16)
        value_grad[0, h] = dot(grad[0, h], probs[spot], NN)[:8].astype(BF16)
        query_grad[0, h] = (dot(key[0, h], pair_grad[0, h], NT)[:8] * 8**-0.5).astype(BF16)

    is_safe = safe[slot] == 1

    @pl.when(is_safe)
    def _():
        for h in range(heads):
            pairs(h // STEP, h % STEP, True)
            if h:
                sums(h - 1, (h - 1) % 2)
        sums(heads - 1, (heads - 1) % 2)

    @pl.when(jnp.logical_not(is_safe))
    def _():
        for h in range(heads):
            pairs(h // STEP, h % STEP, False)
            sums(h, h % 2)


def attend_back(
    safe, scale, pf, cotan, query, key, grad, value, log_total, row_ids, col_ids, per_step
):
    slots, heads, rows, cols = pf.shape

    def by_head(height, width):
        return pl.BlockSpec((1, per_step, height, width), lambda s, g: (s, g, 0, 0))

    return pl.pallas_call(
        backward_body,
        grid=(slots, heads // per_step),
        in_specs=[
            pl.BlockSpec(memory_space=pltpu.SMEM),
            pl.BlockSpec(memory_space=pltpu.SMEM),
            by_head(rows, cols),
            by_head(rows, cols),
            by_head(16, rows),
            by_head(16, cols),
            by_head(16, rows),
            by_head(16, cols),
            pl.BlockSpec((1, per_step // STEP, rows, STEP), lambda s, g: (s, g, 0, 0)),
            pl.BlockSpec((1, 1, rows), lambda s, g: (s, 0, 0)),
            pl.BlockSpec((1, 1, cols), lambda s, g: (s, 0, 0)),
        ],
        out_specs=[
            by_head(rows, cols),
            by_head(rows, cols),
            by_head(8, rows),
            by_head(8, cols),
            by_head(8, cols),
            pl.BlockSpec((16, cols), lambda s, g: (0, 0)),
        ],
        out_shape=[
            jax.ShapeDtypeStruct((slots, heads, rows, cols), BF16),
            jax.ShapeDtypeStruct((slots, heads, rows, cols), BF16),
            jax.ShapeDtypeStruct((slots, heads, 8, rows), BF16),
            jax.ShapeDtypeStruct((slots, heads, 8, cols), BF16),
            jax.ShapeDtypeStruct((slots, heads, 8, cols), BF16),
            jax.ShapeDtypeStruct((16, cols), F32),
        ],
        scratch_shapes=[
            pltpu.VMEM((rows, cols), BF16),
            pltpu.VMEM((rows, cols), BF16),
            pltpu.VMEM((rows, cols), F32),
            pltpu.VMEM((2, rows, cols), BF16),
        ],
        compiler_params=pltpu.CompilerParams(vmem_limit_bytes=60 << 20),
        name="attend_back",
    )(safe, scale, pf, cotan, query, key, grad, value, log_total, row_ids, col_ids)


def flips(sizes):
    found = []
    for axis in ("slot", "blk"):
        bit = 1
        while bit < sizes[axis]:
            found.append((axis, bit))
            bit *= 2
    return found


def swap(values, sizes, axis, bit):
    return lax.ppermute(values, axis, [(i, i ^ bit) for i in range(sizes[axis])])


def butterfly(values, sizes, axes=("slot", "blk")):
    for axis, bit in flips(sizes):
        if axis in axes:
            values = values + swap(values, sizes, axis, bit)
    return values


def step_plan(sizes):
    whole = sizes["slot"] * sizes["blk"]
    blk = sizes["blk"]
    slot_at = lax.axis_index("slot")
    blk_at = lax.axis_index("blk")

    def partner(device, axis, bit):
        s, b = divmod(device, blk)
        return (s ^ bit) * blk + b if axis == "slot" else s * blk + (b ^ bit)

    def bit_of(axis, bit):
        return ((slot_at if axis == "slot" else blk_at) // bit) % 2

    def plain(axis, bit):
        return ([(d, partner(d, axis, bit)) for d in range(whole)], bit_of(axis, bit))

    def mixed(even, odd):
        pairs = [(d, partner(d, *(even if (d // blk) % 2 == 0 else odd))) for d in range(whole)]
        return (pairs, jnp.where(slot_at % 2 == 0, bit_of(*even), bit_of(*odd)))

    steps = flips(sizes)
    core, rest = steps[0], steps[1:]
    near_y, near_x = ("slot", 2), ("blk", 1)
    plan = [plain(*core)]
    if near_y in rest and near_x in rest:
        rest = [step for step in rest if step not in (near_y, near_x)]
        plan += [mixed(near_x, near_y), mixed(near_y, near_x)]
    return plan + [plain(*step) for step in rest]


def sum_all(wide, small, plan):
    joint = ("slot", "blk")
    rows, extra = wide.shape[1], small.shape[1]

    def parcel(wide, small):
        upper = rounded(small)
        parts = [wide.astype(BF16), upper.astype(BF16), (small - upper).astype(BF16)]
        return jnp.concatenate(parts, 1)

    def unpack(values):
        values = values.astype(F32)
        return values[:, :rows], values[:, rows : rows + extra] + values[:, rows + extra :]

    def pick(values, half):
        halves = values.reshape((2, values.shape[0] // 2) + values.shape[1:])
        return lax.dynamic_index_in_dim(halves, half, 0, keepdims=False)

    for pairs, half in plan:
        away = parcel(pick(wide, 1 - half), pick(small, 1 - half))
        came_wide, came_small = unpack(lax.ppermute(away, joint, pairs))
        wide = pick(wide, half) + came_wide
        small = pick(small, half) + came_small
    values = parcel(wide, small)
    for pairs, half in plan[::-1]:
        came = lax.ppermute(values, joint, pairs)
        values = jnp.where(
            half == 0,
            jnp.concatenate([values, came], 0),
            jnp.concatenate([came, values], 0),
        )
    return unpack(values)


def sum_wide(values, sizes, after):
    joint = ("slot", "blk")
    count = sizes["slot"] * sizes["blk"]
    terms = lax.all_to_all(values, joint, 0, 0, tiled=True)
    terms, after = lax.optimization_barrier((terms, after))
    terms = terms.reshape((count, values.shape[0] // count, values.shape[1]))
    total = jnp.sum(terms.astype(F32), axis=0).astype(BF16)
    return lax.all_gather(total, joint, tiled=True), after


def local(
    sizes,
    atom_feats,
    pair_feats,
    type_ids,
    mol_lengths,
    type_table,
    ln1_gain,
    ln1_shift,
    w_query,
    b_query,
    w_key,
    w_value,
    b_value,
    w_out,
    b_out,
    ln2_gain,
    ln2_shift,
    w_up,
    b_up,
    w_down,
    b_down,
    atom_cotan,
    pair_cotan,
):
    slots, rows, width = atom_feats.shape
    heads = pair_feats.shape[1]
    cols = pair_feats.shape[3]
    types = type_table.shape[0]
    blk_at = lax.axis_index("blk")
    row_start = blk_at * rows
    plan = step_plan(sizes)

    def own(values, axis=1):
        return lax.dynamic_slice_in_dim(values, row_start, rows, axis)

    bounds = jnp.cumsum(mol_lengths, axis=1)
    places = jnp.arange(cols, dtype=jnp.int32)
    mol_ids = jnp.sum((places[None, :, None] >= bounds[:, None, :]).astype(jnp.int32), axis=2)
    row_mols = own(mol_ids)
    row_ids = row_mols[:, None, :]
    col_ids = mol_ids[:, None, :]

    first = rounded(type_table)
    second = rounded(type_table - first)
    table = jnp.concatenate([first, second, type_table - first - second], 0).astype(BF16)
    start = row_start.astype(jnp.int32).reshape(1)
    here = blk_at.astype(jnp.int32).reshape(1)

    def line(values):
        return values.reshape(1, -1)

    shared = (table, line(ln1_gain), line(ln1_shift), w_key, w_value, line(b_value))
    asking = (w_query, line(b_query))

    def safe_of(reach):
        furthest = (width // heads) ** (-0.5) * jnp.sqrt(reach[:, 0, 0]) + PAIR_LIMIT
        return (furthest <= SAFE_LOGIT).astype(jnp.int32)

    count = jnp.sum(mol_lengths * mol_lengths).astype(F32).reshape(1, 1)
    if sizes["blk"] == 2:
        there = 1 - here
        came_feats = swap(atom_feats, sizes, "blk", 1)
        came_types = swap(type_ids, sizes, "blk", 1)
        near = [swap(count, sizes, "slot", bit) for bit in (1, 2, 3)]
        base, normed, key_rows, value_rows, reach, far_query, query_rows = prepare(
            here,
            jnp.zeros((1,), jnp.int32),
            atom_feats,
            type_ids[:, None, :],
            shared,
            heads,
            rows,
            cols,
            asking,
        )
        safe = safe_of(reach)
        near, reach = lax.optimization_barrier((near, reach))
        count = count + near[0] + (near[1] + near[2])
        far = [swap(count, sizes, "slot", bit) for bit in range(4, sizes["slot"], 4)]
        base, normed, key_rows, value_rows, reach = prepare(
            there,
            start,
            came_feats,
            came_types[:, None, :],
            shared,
            heads,
            rows,
            cols,
            (far_query, base, normed, key_rows, value_rows),
        )
        safe = safe * safe_of(reach)
        far, safe = lax.optimization_barrier((far, safe))
        pair_total = count + sum(far)
        all_types = jnp.where(
            blk_at == 0,
            jnp.concatenate([type_ids, came_types], 1),
            jnp.concatenate([came_types, type_ids], 1),
        )
    else:
        feats = lax.all_gather(atom_feats, "blk", axis=1, tiled=True)
        all_types = lax.all_gather(type_ids, "blk", axis=1, tiled=True)
        zero = jnp.zeros((1,), jnp.int32)
        base, normed, key_rows, value_rows, reach, _, query_rows = prepare(
            zero,
            start,
            feats,
            all_types[:, None, :],
            shared,
            heads,
            rows,
            cols,
            asking,
        )
        safe = safe_of(reach)
        pair_total = butterfly(count, sizes, ("slot",))
    pen_scale = (2.0 / pair_total).reshape(1)
    weighed, top = attend(
        safe, pair_feats, query_rows, key_rows, value_rows, row_ids, col_ids, 32
    )
    types_row = all_types[:, None, :]

    atom_out, grad_rows, log_total, resid_grad, g_feed, g_b_up, feed_rows = feed(
        here,
        top,
        weighed,
        base,
        atom_cotan,
        w_out,
        line(b_out),
        line(ln2_gain),
        line(ln2_shift),
        w_up,
        line(b_up),
        w_down,
        line(b_down),
    )

    pair_out, pair_grad, query_part, key_part, value_part, pen_tile = attend_back(
        safe,
        pen_scale,
        pair_feats,
        pair_cotan,
        query_rows,
        key_rows,
        grad_rows,
        value_rows,
        log_total,
        row_ids,
        col_ids,
        16,
    )

    devices = sizes["slot"] * sizes["blk"]
    used = types + 9 + g_b_up.shape[1] // width
    halves = sizes["blk"] == 2
    *backs, g_weights, short = finish(
        jnp.concatenate([start, rows - start]),
        query_part,
        key_part,
        value_part,
        base,
        normed,
        types_row,
        resid_grad,
        line(ln1_gain),
        w_query,
        w_key,
        w_value,
        feed_rows,
        g_b_up,
        pen_tile,
        types,
        used + -used % devices,
        halves,
    )
    g_feed, short = sum_wide(g_feed, sizes, short)
    if halves:
        base_grad = backs[0] + swap(backs[1], sizes, "blk", 1).astype(F32)
    else:
        base_grad = resid_grad + lax.psum_scatter(backs[0], "blk", scatter_dimension=1, tiled=True)
    hidden = w_up.shape[1]
    g_w_up = jnp.concatenate(
        [g_feed[at : at + width] for at in range(hidden + width, 2 * hidden + width, width)], 1
    ).astype(F32)
    g_w_down = g_feed[:hidden].astype(F32)
    g_w_out = g_feed[hidden : hidden + width].astype(F32)
    g_weights, packed = sum_all(
        g_weights.reshape(devices, -1, width), short.reshape(devices, -1, width), plan
    )
    g_weights = g_weights.reshape(3 * width, width)
    packed = packed.reshape(-1, width)[:used]
    at = types
    (
        g_ln1_gain,
        g_ln1_shift,
        g_b_query,
        g_b_value,
        g_b_out,
        g_ln2_gain,
        g_ln2_shift,
        g_b_down,
    ) = (packed[at + i] for i in range(8))
    return (
        atom_out,
        pair_out,
        packed[-1, 0],
        base_grad.astype(BF16),
        pair_grad,
        packed[:types],
        g_ln1_gain,
        g_ln1_shift,
        g_weights[:width],
        g_b_query,
        g_weights[width : 2 * width],
        g_weights[2 * width :],
        g_b_value,
        g_w_out,
        g_b_out,
        g_ln2_gain,
        g_ln2_shift,
        g_w_up,
        packed[at + 8 : used - 1].reshape(-1),
        g_w_down,
        g_b_down,
    )


def solution(mesh):
    atoms = P("slot", "blk", None)
    pairs = P("slot", None, "blk", None)
    sizes = {axis: mesh.shape[axis] for axis in ("slot", "blk")}
    return jax.shard_map(
        functools.partial(local, sizes),
        mesh=mesh,
        in_specs=(atoms, pairs, P("slot", "blk"), P("slot", None))
        + (P(),) * 16
        + (atoms, pairs),
        out_specs=(atoms, pairs, P(), atoms, pairs) + (P(),) * 16,
        check_vma=False,
    )
```
